32 devices in a mesh: parts: 2 (over y), seq: 4 (over z), head: 2 (over x), hgt: 2 (over core).
Axes of the slice: x: 2, y: 2, z: 4, core: 2. Of those that a mesh axis runs over, the one named last changes fastest.
Arguments:
- queries: bfloat16 [16, 8, 24, 2048], P(('parts', 'seq'), 'hgt', None, 'head'), parts along dimension 0
- key_rows: bfloat16 [16, 8, 24, 2048], P(('parts', 'seq'), 'hgt', None, 'head'), parts along dimension 0
- value_rows: bfloat16 [16, 8, 24, 2048], P(('parts', 'seq'), 'hgt', None, 'head'), parts along dimension 0, may hold values from -6 to 6
- out_grad: bfloat16 [16, 8, 24, 3072], P(('parts', 'seq'), 'hgt', None, 'head'), parts along dimension 0, may hold values from -6 to 6
- w_out: bfloat16 [3072, 2048], P(None, 'head'), may hold values from -0.109375 to 0.109375
- text_keys: bfloat16 [512, 2048], P('parts', 'head'), parts along dimension 0, may hold values from -6 to 6
- text_values: bfloat16 [512, 2048], P('parts', 'head'), parts along dimension 0, may hold values from -6 to 6
- text_count: int32 [2], P('parts'), parts along dimension 0, may hold values from 64 to 256
- window_start: int32 [16, 4, 3, 3], P('parts'), parts along dimension 0, may hold values from 0 to 5, as said below
Outputs:
- grad_query: bfloat16 [16, 8, 24, 2048], P(('parts', 'seq'), 'hgt', None, 'head'), parts along dimension 0
- grad_key: bfloat16 [16, 8, 24, 2048], P(('parts', 'seq'), 'hgt', None, 'head'), parts along dimension 0
- grad_value: bfloat16 [16, 8, 24, 2048], P(('parts', 'seq'), 'hgt', None, 'head'), parts along dimension 0
- grad_w_out: float32 [6144, 2048], P(('parts', 'seq', 'hgt'), 'head'), parts along dimension 0
- grad_text_key: float32 [512, 2048], P('parts', 'head'), parts along dimension 0
- grad_text_value: float32 [512, 2048], P('parts', 'head'), parts along dimension 0
The draws below stay inside these ranges and needn't reach their ends.
There are 2 independent parts, one for each index of `parts`. The reference program is written for one: setup_inputs(seed, part) draws one part's arguments, and reference() takes and returns one part's arrays. A program takes and returns all parts, laid end to end along the dimension named above; an argument that names none is the same for every part. Nothing has to cross between parts.
Inputs may be any that keep to these rules, and one draw needn't show every extreme that they name: window_start[a, b, c] names the first frame, height tile and width tile of the window of the tile at frame a, height tile b, width tile c; each window lies inside the clip and contains that tile. The first text_count[0] text slots are valid.
All inputs are finite; a program needn't handle non-finite values.
Results may differ from the reference program's by a relative error of at most 0.012.
Values may be sent and summed in bfloat16 or wider, within the bound.
A program may use at most 128 MiB of HBM per device.

```python
import jax
import jax.numpy as jnp
from jax import lax

D = 3072
HDIM = 128
HEADS = 16
TXT = 256
TH = 2
TW = 8
WIN = 3
W = 24
NF = 8
NH = 8


def paired_fields(key):
    shape = (NF, NH, W, HEADS * HDIM)
    base_query = jnp.clip(jax.random.normal(jax.random.fold_in(key, 11), shape, jnp.float32), -4.0, 4.0)
    base_key = jnp.clip(jax.random.normal(jax.random.fold_in(key, 12), shape, jnp.float32), -4.0, 4.0)
    query_field = base_query
    key_field = base_key
    return (query_field, key_field)


def draw_queries(key, part):
    return paired_fields(key)[0].astype(jnp.bfloat16)


def draw_key_rows(key, part):
    return paired_fields(key)[1].astype(jnp.bfloat16)


def axis_start(key, count, shape, axis):
    tile = lax.broadcasted_iota(jnp.int32, shape, axis)
    offset = jax.random.randint(key, shape, -1, 2)
    return jnp.clip(tile - 1 + offset, 0, count - WIN)


def draw_window_start(key, part):
    shape = (NF, NH // TH, W // TW)
    components = [axis_start(jax.random.fold_in(key, 21 + number), shape[number], shape, number) for number in range(3)]
    return jnp.stack(components, axis=-1).astype(jnp.int32)


def steps_of(rng, shape, cuts, low, high):
    gain, own = 1.0, jax.random.fold_in(rng, 6)
    for dim, blocks in cuts:
        heights = jnp.exp(jax.random.uniform(jax.random.fold_in(own, dim), (blocks,), jnp.float32, low / len(cuts), high / len(cuts)))
        gain = gain * jnp.repeat(heights, shape[dim] // blocks).reshape([-1 if axis == dim else 1 for axis in range(len(shape))])
    return gain


def gaussian(rng, dims, deviation, bound, cuts=(), kind=jnp.bfloat16):
    result = deviation * jax.random.normal(rng, dims, jnp.float32)
    if cuts:
        result = result * steps_of(rng, dims, cuts, -0.22, 0.18)
    return jnp.clip(result, -bound, bound).astype(kind)


def setup_inputs(seed: int = 0, part: int = 0) -> dict:
    seeds = jax.random.split(jax.random.key(seed), 10)
    part_keys = jax.random.split(jax.random.fold_in(seeds[9], part), 10)
    return {
        "queries": draw_queries(jax.random.fold_in(jax.random.fold_in(seeds[9], part), 71), part),
        "key_rows": draw_key_rows(jax.random.fold_in(jax.random.fold_in(seeds[9], part), 71), part),
        "value_rows": gaussian(part_keys[2], (NF, NH, W, HEADS * HDIM), 1.0, 6.0, ((0, 4), (1, 2), (3, 2))),
        "out_grad": gaussian(part_keys[3], (NF, NH, W, D), 1.0, 6.0, ((0, 4), (1, 2), (3, 2))),
        "w_out": gaussian(seeds[4], (D, HEADS * HDIM), D ** -0.5, 0.109375, ((1, 2),)),
        "text_keys": gaussian(part_keys[5], (TXT, HEADS * HDIM), 1.0, 6.0, ((1, 2),)),
        "text_values": gaussian(part_keys[6], (TXT, HEADS * HDIM), 1.0, 6.0, ((1, 2),)),
        "text_count": jax.random.randint(part_keys[7], (1,), TXT // 4, TXT + 1).astype(jnp.int32),
        "window_start": draw_window_start(jax.random.fold_in(jax.random.fold_in(seeds[9], part), 71), part),
    }


def rounded(value):
    return lax.optimization_barrier(value.astype(jnp.bfloat16)).astype(jnp.float32)


def split_heads(value):
    return value.astype(jnp.float32).reshape(-1, HEADS, HDIM).transpose(1, 0, 2)


def reference(queries, key_rows, value_rows, out_grad, w_out, text_keys, text_values, text_count, window_start):
    reach = WIN - 1
    span = 2 * reach + 1
    plane = NH * W
    col_total = HEADS * HDIM
    score_scale = jnp.float32(HDIM ** -0.5)
    grad_o = jnp.dot(out_grad.reshape(NF * plane, D), w_out, preferred_element_type=jnp.float32)
    grad_o = grad_o.astype(jnp.bfloat16).reshape(NF, NH, W, col_total)
    padding = ((reach, reach), (0, 0), (0, 0), (0, 0))
    key_pad = jnp.pad(key_rows, padding)
    value_pad = jnp.pad(value_rows, padding)
    own_index = jnp.arange(plane, dtype=jnp.int32)
    own_row = own_index // W
    own_col = own_index % W
    far_index = jnp.arange(span * plane, dtype=jnp.int32)
    far_slab = far_index // plane
    far_tile_row = ((far_index // W) % NH) // TH
    far_tile_col = (far_index % W) // TW
    text_open = (jnp.arange(TXT, dtype=jnp.int32) < text_count[0])[None, None, :]
    text_key_h = split_heads(text_keys)
    text_value_h = split_heads(text_values)

    def frame_step(carry, frame):
        acc_key, acc_value, text_gk, text_gv, proj = carry
        starts = window_start[frame][own_row // TH, own_col // TW]
        far_frame = frame - reach + far_slab
        inside = ((far_frame[None, :] >= starts[:, 0:1]) & (far_frame[None, :] < starts[:, 0:1] + WIN)
                  & (far_tile_row[None, :] >= starts[:, 1:2]) & (far_tile_row[None, :] < starts[:, 1:2] + WIN)
                  & (far_tile_col[None, :] >= starts[:, 2:3]) & (far_tile_col[None, :] < starts[:, 2:3] + WIN))
        query_h = split_heads(queries[frame])
        grad_h = split_heads(grad_o[frame])
        key_h = split_heads(lax.dynamic_slice_in_dim(key_pad, frame, span, 0))
        value_h = split_heads(lax.dynamic_slice_in_dim(value_pad, frame, span, 0))
        score_w = jnp.einsum("hqd,hkd->hqk", query_h, key_h) * score_scale
        score_t = jnp.einsum("hqd,hkd->hqk", query_h, text_key_h) * score_scale
        score_w = jnp.where(inside[None], score_w, -jnp.inf)
        score_t = jnp.where(text_open, score_t, -jnp.inf)
        row_top = jnp.maximum(jnp.max(score_w, axis=2), jnp.max(score_t, axis=2))
        total = jnp.sum(jnp.exp(score_w - row_top[..., None]), axis=2) + jnp.sum(jnp.exp(score_t - row_top[..., None]), axis=2)
        log_total = row_top + jnp.log(total)
        prob_w = jnp.exp(score_w - log_total[..., None])
        prob_t = jnp.exp(score_t - log_total[..., None])
        pb_w = rounded(prob_w)
        pb_t = rounded(prob_t)
        attn_out = rounded(jnp.einsum("hqk,hkd->hqd", pb_w, value_h) + jnp.einsum("hqk,hkd->hqd", pb_t, text_value_h))
        row_delta = jnp.sum(grad_h * attn_out, axis=2)
        dp_w = jnp.einsum("hqd,hkd->hqk", grad_h, value_h)
        dp_t = jnp.einsum("hqd,hkd->hqk", grad_h, text_value_h)
        ds_w = rounded(prob_w * (dp_w - row_delta[..., None]))
        ds_t = rounded(prob_t * (dp_t - row_delta[..., None]))
        grad_q = score_scale * (jnp.einsum("hqk,hkd->hqd", ds_w, key_h) + jnp.einsum("hqk,hkd->hqd", ds_t, text_key_h))
        grad_q = grad_q.transpose(1, 0, 2).reshape(NH, W, col_total).astype(jnp.bfloat16)
        key_part = (score_scale * jnp.einsum("hqk,hqd->hkd", ds_w, query_h)).transpose(1, 0, 2).reshape(span, NH, W, col_total)
        value_part = jnp.einsum("hqk,hqd->hkd", pb_w, grad_h).transpose(1, 0, 2).reshape(span, NH, W, col_total)
        zero = jnp.zeros((), jnp.int32)
        acc_key = lax.dynamic_update_slice(acc_key, lax.dynamic_slice_in_dim(acc_key, frame, span, 0) + key_part, (frame, zero, zero, zero))
        acc_value = lax.dynamic_update_slice(acc_value, lax.dynamic_slice_in_dim(acc_value, frame, span, 0) + value_part, (frame, zero, zero, zero))
        text_gk = text_gk + score_scale * jnp.einsum("hqk,hqd->hkd", ds_t, query_h)
        text_gv = text_gv + jnp.einsum("hqk,hqd->hkd", pb_t, grad_h)
        out_flat = attn_out.transpose(1, 0, 2).reshape(plane, col_total).astype(jnp.bfloat16)
        proj = proj + jnp.dot(out_grad[frame].reshape(plane, D).T, out_flat, preferred_element_type=jnp.float32)
        return (acc_key, acc_value, text_gk, text_gv, proj), grad_q

    start_carry = (jnp.zeros((NF + 2 * reach, NH, W, col_total), jnp.float32),
                   jnp.zeros((NF + 2 * reach, NH, W, col_total), jnp.float32),
                   jnp.zeros((HEADS, TXT, HDIM), jnp.float32),
                   jnp.zeros((HEADS, TXT, HDIM), jnp.float32),
                   jnp.zeros((D, col_total), jnp.float32))
    final, grad_query = lax.scan(frame_step, start_carry, jnp.arange(NF, dtype=jnp.int32))
    acc_key, acc_value, text_gk, text_gv, proj = final
    grad_key = acc_key[reach:reach + NF].astype(jnp.bfloat16)
    grad_value = acc_value[reach:reach + NF].astype(jnp.bfloat16)
    grad_text_key = text_gk.transpose(1, 0, 2).reshape(TXT, col_total)
    grad_text_value = text_gv.transpose(1, 0, 2).reshape(TXT, col_total)
    return (grad_query, grad_key, grad_value, proj, grad_text_key, grad_text_value)
```

```python
import functools

import jax
import jax.numpy as jnp
from jax import lax
from jax.experimental import pallas as pl
from jax.experimental.pallas import tpu as pltpu
from jax.sharding import PartitionSpec as P

HDIM = 128
TH = 2
TW = 8
WIN = 3

F32 = jnp.float32
BF16 = jnp.bfloat16


def contract(a, b, dims):
    return lax.dot_general(a, b, (dims, ((), ())), preferred_element_type=F32)


def head_kernel(bias_ref, q_ref, k_ref, v_ref, tk_ref, tv_ref, do_ref,
                dq_ref, o_ref, dk_ref, dv_ref, dtk_ref, dtv_ref):
    scale = HDIM ** -0.5
    ext = k_ref.shape[0]
    q, do, k, v, tk, tv = (r[...] for r in (q_ref, do_ref, k_ref, v_ref, tk_ref, tv_ref))
    s_w = contract(q, k, ((1,), (1,))) * scale + bias_ref[:, :ext]
    s_t = contract(q, tk, ((1,), (1,))) * scale + bias_ref[:, ext:]
    top = jnp.maximum(jnp.max(s_w, axis=1, keepdims=True), jnp.max(s_t, axis=1, keepdims=True))
    e_w = jnp.exp(s_w - top)
    e_t = jnp.exp(s_t - top)
    total = jnp.sum(e_w, axis=1, keepdims=True) + jnp.sum(e_t, axis=1, keepdims=True)
    inv = 1.0 / total
    p_w = e_w * inv
    p_t = e_t * inv
    pb_w = p_w.astype(BF16)
    pb_t = p_t.astype(BF16)
    o = (contract(pb_w, v, ((1,), (0,))) + contract(pb_t, tv, ((1,), (0,)))).astype(BF16)
    o_ref[...] = o
    delta = jnp.sum(do.astype(F32) * o.astype(F32), axis=1, keepdims=True)
    ds_w = (p_w * (contract(do, v, ((1,), (1,))) - delta)).astype(BF16)
    ds_t = (p_t * (contract(do, tv, ((1,), (1,))) - delta)).astype(BF16)
    dq = contract(ds_w, k, ((1,), (0,))) + contract(ds_t, tk, ((1,), (0,)))
    dq_ref[...] = (dq * scale).astype(BF16)
    dk_ref[...] = (contract(ds_w, q, ((0,), (0,))) * scale).astype(BF16)
    dv_ref[...] = contract(pb_w, do, ((0,), (0,))).astype(BF16)
    dtk_ref[...] = contract(ds_t, q, ((0,), (0,))) * scale
    dtv_ref[...] = contract(pb_t, do, ((0,), (0,)))


def attention(bias, q, k, v, tk, tv, do):
    rows, cols = q.shape
    ext = k.shape[0]
    txt = tk.shape[0]
    heads = cols // HDIM

    def per_head(n):
        return pl.BlockSpec((n, HDIM), lambda h: (0, h))

    return pl.pallas_call(
        head_kernel,
        grid=(heads,),
        in_specs=[pl.BlockSpec(bias.shape, lambda h: (0, 0)), per_head(rows), per_head(ext), per_head(ext),
                  per_head(txt), per_head(txt), per_head(rows)],
        out_specs=[per_head(rows), per_head(rows), per_head(ext), per_head(ext), per_head(txt), per_head(txt)],
        out_shape=[
            jax.ShapeDtypeStruct((rows, cols), BF16),
            jax.ShapeDtypeStruct((rows, cols), BF16),
            jax.ShapeDtypeStruct((ext, cols), BF16),
            jax.ShapeDtypeStruct((ext, cols), BF16),
            jax.ShapeDtypeStruct((txt, cols), F32),
            jax.ShapeDtypeStruct((txt, cols), F32),
        ],
        compiler_params=pltpu.CompilerParams(vmem_limit_bytes=48 * 1024 * 1024),
        name="heads",
    )(bias, q, k, v, tk, tv, do)


def make_bias(window_start, text_count, frames, height, col_count, full_h, txt):
    frame_first = lax.axis_index("seq") * frames
    row_first = lax.axis_index("hgt") * height
    halves = full_h // height
    rows = frames * height * col_count
    tiles_h, tiles_w = full_h // TH, col_count // TW
    own = jnp.arange(rows, dtype=jnp.int32)
    starts = lax.dynamic_slice_in_dim(window_start, frame_first, frames, 0)
    starts = lax.dynamic_slice_in_dim(starts, lax.axis_index("hgt") * (height // TH), height // TH, 1)
    starts = jnp.repeat(jnp.repeat(starts, TH, axis=1), TW, axis=2).reshape(rows, 3)
    key = jnp.arange(3 * halves * rows, dtype=jnp.int32)
    block = key // rows
    inner = key % rows
    kf = frame_first + (block // halves - 1) * frames + inner // (height * col_count)
    kr = ((block % halves) * height + inner // col_count % height) // TH
    kc = inner % col_count // TW
    ok = True
    for n, pos in enumerate((kf, kr, kc)):
        low = starts[:, n:n + 1]
        ok = ok & (pos[None] >= low) & (pos[None] < low + WIN)
    text_ok = jnp.broadcast_to((jnp.arange(txt, dtype=jnp.int32) < text_count[0])[None], (rows, txt))
    ok = jnp.concatenate([ok, text_ok], axis=1)
    return jnp.where(ok, F32(0), F32(-jnp.inf))


def per_device(
    queries, key_rows, value_rows, out_grad, w_out, text_keys, text_values, text_count, window_start
):
    frames, height, col_count, columns = queries.shape
    rows = frames * height * col_count
    halves = lax.axis_size("hgt")
    nz = lax.axis_size("seq")
    txt = text_keys.shape[0]
    up = [(i, i + 1) for i in range(nz - 1)]
    down = [(i + 1, i) for i in range(nz - 1)]
    grad_full = lax.all_gather(out_grad.reshape(rows, -1), "head", axis=1, tiled=True)

    def halo(x):
        x = x.reshape(rows, columns)
        slabs = jnp.stack([lax.ppermute(x, "seq", up), x, lax.ppermute(x, "seq", down)])
        return lax.all_gather(slabs, "hgt", axis=1).reshape(3 * halves * rows, columns)

    k_ext = halo(key_rows)
    v_ext = halo(value_rows)
    bias = make_bias(window_start, text_count, frames, height, col_count, height * halves, txt)
    grad_o = jnp.dot(grad_full, w_out, preferred_element_type=F32).astype(BF16)
    og = lax.all_to_all(grad_full, ("seq", "hgt"), split_axis=1, concat_axis=0, tiled=True)
    dq, o, dk, dv, dtk, dtv = attention(
        bias, queries.reshape(rows, columns), k_ext, v_ext, text_keys, text_values, grad_o
    )
    o_all = lax.all_gather(o, ("seq", "hgt"), axis=0, tiled=True)
    me = lax.axis_index("hgt")

    def back(part):
        part = part.reshape(3, halves, rows, columns)
        mine = lax.dynamic_index_in_dim(part, me, 1, keepdims=False)
        other = lax.dynamic_index_in_dim(part, 1 - me, 1, keepdims=False)
        got = lax.ppermute(other, "hgt", [(0, 1), (1, 0)])
        mine = mine.astype(F32) + got.astype(F32)
        low = lax.ppermute(mine[0].astype(BF16), "seq", down)
        high = lax.ppermute(mine[2].astype(BF16), "seq", up)
        mine = mine[1] + low.astype(F32) + high.astype(F32)
        return mine.astype(BF16).reshape(queries.shape)

    grad_key = back(dk)
    grad_value = back(dv)
    grad_text_key, grad_text_value = lax.psum((dtk, dtv), ("seq", "hgt"))
    grad_w_out = contract(og, o_all, ((0,), (0,)))
    return (dq.reshape(queries.shape), grad_key, grad_value, grad_w_out, grad_text_key, grad_text_value)


def solution(mesh):
    tok = P(("parts", "seq"), "hgt", None, "head")
    return jax.shard_map(
        per_device,
        mesh=mesh,
        in_specs=(tok, tok, tok, tok, P(None, "head"), P("parts", "head"), P("parts", "head"),
                  P("parts"), P("parts", None, None, None)),
        out_specs=(tok, tok, tok, P(("parts", "seq", "hgt"), "head"), P("parts", "head"), P("parts", "head")),
        check_vma=False,
    )
```

```python
import functools

import jax
import jax.numpy as jnp
import numpy as np
from jax import lax
from jax.experimental import pallas as pl
from jax.experimental.pallas import tpu as pltpu
from jax.sharding import PartitionSpec as P

HDIM = 128
TH = 2
TW = 8
WIN = 3

F32 = jnp.float32
BF16 = jnp.bfloat16
MESH = pl.DeviceIdType.MESH


def contract(a, b, dims):
    return lax.dot_general(a, b, (dims, ((), ())), preferred_element_type=F32)


def body(cfg, window, count, key_table, tile_table, q_in, k_in, v_in, og_in, w_in, tk_in, tv_in,
         dq_out, dk_out, dv_out, gw_out, dtk_out, dtv_out,
         q, tk, tv, w, do, bias, gfull, stage, a_all, k_ext, v_ext, dk_part, dv_part, k_got, v_got,
         k_sum, v_sum, k_mid, v_mid, k_ret, v_ret, o_all, t_part, t_got, t_sum, t_red, t_all,
         loc, og_s, og_r, kv_s, kv_r, kp_s, kp_r, a_s, a_r, pr_s, pr_r, rz_s, rz_r,
         o_s, o_r, of_s, of_r, tp_s, tp_r, ts_s, ts_r, tg_s, tg_r, tf_s, tf_r):
    nz, nx, rows, cols, groups, frames, height, width = cfg
    txt = tk_in.shape[0]
    slot = og_in.shape[1]
    chunk = stage.shape[2]
    share = txt // nz
    ext = 6 * rows
    heads = cols // HDIM
    per = heads // groups
    gcols = per * HDIM
    scale = HDIM ** -0.5
    y, z, x, c = (lax.axis_index(n) for n in ("parts", "seq", "head", "hgt"))
    partner = (y, z, x, 1 - c)
    up = (y, lax.rem(z + 1, nz), x, c)
    down = (y, lax.rem(z + nz - 1, nz), x, c)
    has_up = z < nz - 1
    has_down = z > 0

    def seq_peer(step):
        zt = lax.rem(z + step, nz)
        return zt, (y, zt, x, c)

    def copy(src, dst, s, r, dev):
        return pltpu.make_async_remote_copy(
            src_ref=src, dst_ref=dst, send_sem=s, recv_sem=r, device_id=dev, device_id_type=MESH)

    def got(dst, s, r):
        copy(dst, dst, s, r, partner).wait_recv()

    def row_block(n, size):
        return pl.ds(pl.multiple_of(n * size, 16), size)

    def key_rows(half, slab):
        return row_block(half * 3 + slab, rows)

    sent = []

    def send(when, make):
        if when is None:
            make().start()
        else:
            pl.when(when)(lambda: make().start())
        sent.append((when, make))

    locals_ = [
        pltpu.make_async_copy(w_in, w, loc.at[0]),
        pltpu.make_async_copy(q_in, q, loc.at[1]),
        pltpu.make_async_copy(tk_in, tk, loc.at[2]),
        pltpu.make_async_copy(tv_in, tv, loc.at[3]),
        pltpu.make_async_copy(k_in, k_ext.at[key_rows(c, 1)], loc.at[4]),
        pltpu.make_async_copy(v_in, v_ext.at[key_rows(c, 1)], loc.at[5]),
        pltpu.make_async_copy(og_in, gfull.at[x], loc.at[6]),
    ]
    locals_[6].start()
    for n in range(6):
        locals_[n].start()

    barrier = pltpu.get_barrier_semaphore()
    for step in range(nz):
        zt, dev = seq_peer(step)
        if step:
            pl.semaphore_signal(barrier, inc=1, device_id=dev, device_id_type=MESH)
        pl.semaphore_signal(barrier, inc=1, device_id=(y, zt, x, 1 - c), device_id_type=MESH)
    for step in range(1, nx):
        pl.semaphore_signal(barrier, inc=1, device_id=(y, z, lax.rem(x + step, nx), c), device_id_type=MESH)
    pl.semaphore_wait(barrier, 2 * nz - 1 + nx - 1)

    for step in range(1, nx):
        send(None, lambda step=step: copy(og_in, gfull.at[x], og_s.at[step], og_r.at[step],
                                          (y, z, lax.rem(x + step, nx), c)))
    for n, (src, dst) in enumerate(((k_in, k_ext), (v_in, v_ext))):
        send(has_up, lambda n=n, src=src, dst=dst: copy(
            src, dst.at[key_rows(c, 0)], kv_s.at[0, n], kv_r.at[0, n], up))
        send(has_down, lambda n=n, src=src, dst=dst: copy(
            src, dst.at[key_rows(c, 2)], kv_s.at[1, n], kv_r.at[1, n], down))
    for n, (src, dst) in enumerate(((k_in, k_ext), (v_in, v_ext))):
        send(None, lambda n=n, src=src, dst=dst: copy(
            src, dst.at[key_rows(c, 1)], kp_s.at[1, n], kp_r.at[1, n], partner))

    @pl.when(jnp.logical_not(has_down))
    def _():
        for ref in (k_ext, v_ext):
            for half in range(2):
                ref[pl.ds(half * 3 * rows, rows), :] = jnp.zeros((rows, cols), BF16)
        for ref in (k_ret, v_ret):
            ref[0] = jnp.zeros((rows, cols), BF16)

    @pl.when(jnp.logical_not(has_up))
    def _():
        for ref in (k_ext, v_ext):
            for half in range(2):
                ref[pl.ds((half * 3 + 2) * rows, rows), :] = jnp.zeros((rows, cols), BF16)
        for ref in (k_ret, v_ret):
            ref[1] = jnp.zeros((rows, cols), BF16)

    tile_id = tile_table[...]
    tiles_h, tiles_w = 2 * height // TH, width // TW
    ok = None
    for n in range(3):
        low = jnp.zeros((rows, 1), jnp.int32)
        t = 0
        for f in range(frames):
            for r in range(height // TH):
                for e in range(tiles_w):
                    at = (((z * frames + f) * tiles_h + c * (height // TH) + r) * tiles_w + e) * 3 + n
                    low = jnp.where(tile_id == t, window[at], low)
                    t += 1
        pos = key_table[n:n + 1, :]
        if n == 0:
            pos = pos + z * frames
        term = (pos >= low) & (pos < low + WIN)
        ok = term if ok is None else ok & term
    bias[:, :ext] = jnp.where(ok, F32(0), F32(-jnp.inf))
    place = lax.broadcasted_iota(jnp.int32, (rows, txt), 1)
    bias[:, ext:] = jnp.where(place < count[0], F32(0), F32(-jnp.inf))

    locals_[0].wait()
    locals_[6].wait()

    def term_of(xs):
        return contract(gfull[xs], w[row_block(xs, slot), :], ((1,), (0,)))

    total = term_of(x)
    for step in range(1, nx):
        xs = lax.rem(x + nx - step, nx)
        got(gfull.at[xs], og_s.at[step], og_r.at[step])
    per_slot = slot // chunk
    for j in range(2 * nz):
        stage[j] = gfull[j // per_slot, :, (j % per_slot) * chunk:(j % per_slot + 1) * chunk]
    for step in range(1, nz):
        for ct in range(2):
            zt = lax.rem(z + step, nz)
            send(None, lambda zt=zt, step=step, ct=ct: copy(
                stage.at[zt * 2 + ct], a_all.at[z, row_block(c, rows), :], a_s.at[step, ct], a_r.at[step, c],
                (y, zt, x, ct)))
    send(None, lambda: copy(stage.at[z * 2 + 1 - c], a_all.at[z, row_block(c, rows), :], a_s.at[0, 0], a_r.at[0, c],
                            partner))
    a_all[z, row_block(c, rows), :] = stage[z * 2 + c]

    for slab, there, cond in ((0, 0, has_down), (2, 1, has_up)):
        @pl.when(cond)
        def _():
            for n, dst in enumerate((k_ext, v_ext)):
                got(dst.at[key_rows(c, slab)], kv_s.at[there, n], kv_r.at[there, n])
        for n, dst in enumerate((k_ext, v_ext)):
            send(cond, lambda n=n, dst=dst, slab=slab: copy(
                dst.at[key_rows(c, slab)], dst.at[key_rows(c, slab)], kp_s.at[slab, n], kp_r.at[slab, n], partner))

    for step in range(1, nx):
        total = total + term_of(lax.rem(x + nx - step, nx))
    do[...] = total.astype(BF16)

    for n in range(1, 6):
        locals_[n].wait()
    for slab, cond in ((0, has_down), (1, None), (2, has_up)):
        def arrive(slab=slab):
            for n, dst in enumerate((k_ext, v_ext)):
                got(dst.at[key_rows(1 - c, slab)], kp_s.at[slab, n], kp_r.at[slab, n])
        if cond is None:
            arrive()
        else:
            pl.when(cond)(arrive)

    def reduce_group(g):
        lanes = pl.ds(g * gcols, gcols)
        for n, (part, have, mid, summed, ret) in enumerate((
                (dk_part, k_got, k_mid, k_sum, k_ret), (dv_part, v_got, v_mid, v_sum, v_ret))):
            got(have.at[:, lanes], pr_s.at[g, n], pr_r.at[g, n])
            for slab in range(3):
                value = (part[key_rows(c, slab), lanes].astype(F32)
                         + have[pl.ds(slab * rows, rows), lanes].astype(F32))
                if slab == 1:
                    mid[:, lanes] = value
                else:
                    summed[slab // 2, :, lanes] = value.astype(BF16)
            send(has_down, lambda n=n, summed=summed, ret=ret: copy(
                summed.at[0, :, lanes], ret.at[1, :, lanes], rz_s.at[0, g, n], rz_r.at[0, g, n], down))
            send(has_up, lambda n=n, summed=summed, ret=ret: copy(
                summed.at[1, :, lanes], ret.at[0, :, lanes], rz_s.at[1, g, n], rz_r.at[1, g, n], up))

    for g in range(groups):
        for h in range(g * per, (g + 1) * per):
            at = pl.ds(h * HDIM, HDIM)
            qh, doh, kh, vh, tkh, tvh = q[:, at], do[:, at], k_ext[:, at], v_ext[:, at], tk[:, at], tv[:, at]
            s_w = contract(qh, kh, ((1,), (1,))) * scale + bias[:, :ext]
            s_t = contract(qh, tkh, ((1,), (1,))) * scale + bias[:, ext:]
            top = jnp.maximum(jnp.max(s_w, axis=1, keepdims=True), jnp.max(s_t, axis=1, keepdims=True))
            e_w = jnp.exp(s_w - top)
            e_t = jnp.exp(s_t - top)
            inv = 1.0 / (jnp.sum(e_w, axis=1, keepdims=True) + jnp.sum(e_t, axis=1, keepdims=True))
            p_w = e_w * inv
            p_t = e_t * inv
            pb_w = p_w.astype(BF16)
            pb_t = p_t.astype(BF16)
            oh = (contract(pb_w, vh, ((1,), (0,))) + contract(pb_t, tvh, ((1,), (0,)))).astype(BF16)
            o_all[z, row_block(c, rows), at] = oh
            delta = jnp.sum(doh.astype(F32) * oh.astype(F32), axis=1, keepdims=True)
            ds_w = (p_w * (contract(doh, vh, ((1,), (1,))) - delta)).astype(BF16)
            ds_t = (p_t * (contract(doh, tvh, ((1,), (1,))) - delta)).astype(BF16)
            dq = contract(ds_w, kh, ((1,), (0,))) + contract(ds_t, tkh, ((1,), (0,)))
            dq_out[:, at] = (dq * scale).astype(BF16)
            dk_part[:, at] = (contract(ds_w, qh, ((0,), (0,))) * scale).astype(BF16)
            dv_part[:, at] = contract(pb_w, doh, ((0,), (0,))).astype(BF16)
            t_part[0, :, at] = (contract(ds_t, qh, ((0,), (0,))) * scale).astype(BF16)
            t_part[1, :, at] = contract(pb_t, doh, ((0,), (0,))).astype(BF16)
        lanes = pl.ds(g * gcols, gcols)
        for n, (part, have) in enumerate(((dk_part, k_got), (dv_part, v_got))):
            send(None, lambda n=n, part=part, have=have, g=g, lanes=lanes: copy(
                part.at[row_block(1 - c, 3 * rows), lanes], have.at[:, lanes], pr_s.at[g, n], pr_r.at[g, n], partner))
        for step in range(nz):
            zt, dev = seq_peer(step)
            mine = o_all.at[z, row_block(c, rows), lanes]
            if step:
                send(None, lambda mine=mine, g=g, step=step, dev=dev: copy(
                    mine, mine, o_s.at[g, step], o_r.at[g, step], dev))
            else:
                send(None, lambda mine=mine, g=g: copy(mine, mine, of_s.at[g, 0], of_r.at[g, 0], partner))
        if g:
            reduce_group(g - 1)

    send(None, lambda: copy(t_part.at[1 - c], t_got, tp_s, tp_r, partner))
    reduce_group(groups - 1)
    got(t_got, tp_s, tp_r)
    t_sum[...] = (t_part[c].astype(F32) + t_got[...].astype(F32)).astype(BF16)
    for step in range(1, nz):
        zt, dev = seq_peer(step)
        send(None, lambda step=step, zt=zt, dev=dev: copy(
            t_sum.at[row_block(zt, share)], t_red.at[row_block(z, share)], ts_s.at[step], ts_r.at[step], dev))

    for step in range(1, nz):
        zf = lax.rem(z + nz - step, nz)
        for g in range(groups):
            lanes = pl.ds(g * gcols, gcols)
            theirs = o_all.at[zf, row_block(c, rows), lanes]
            got(theirs, o_s.at[g, step], o_r.at[g, step])
            send(None, lambda theirs=theirs, g=g, step=step: copy(
                theirs, theirs, of_s.at[g, step], of_r.at[g, step], partner))

    value = t_sum[row_block(z, share), :].astype(F32)
    for step in range(1, nz):
        zf = lax.rem(z + nz - step, nz)
        got(t_red.at[row_block(zf, share)], ts_s.at[step], ts_r.at[step])
        value = value + t_red[row_block(zf, share), :].astype(F32)
    t_all[c, row_block(z, share), :] = value.astype(BF16)
    own_text = t_all.at[c, row_block(z, share)]
    for step in range(nz):
        zt, dev = seq_peer(step)
        if step:
            send(None, lambda step=step, dev=dev: copy(own_text, own_text, tg_s.at[step], tg_r.at[step], dev))
        else:
            send(None, lambda: copy(own_text, own_text, tf_s.at[0], tf_r.at[0], partner))

    for step in range(nz):
        zf = lax.rem(z + nz - step, nz)
        if step == 0:
            got(a_all.at[z, row_block(1 - c, rows), :], a_s.at[0, 0], a_r.at[0, 1 - c])
        else:
            for cf in range(2):
                got(a_all.at[zf, pl.ds(cf * rows, rows), :], a_s.at[step, cf], a_r.at[step, cf])
        for g in range(groups):
            got(o_all.at[zf, row_block(1 - c, rows), pl.ds(g * gcols, gcols)], of_s.at[g, step], of_r.at[g, step])
        part = contract(a_all[zf], o_all[zf], ((0,), (0,)))
        if step == 0:
            gw_out[...] = part
        else:
            gw_out[...] += part

    for slab, there, cond in ((0, 1, has_down), (1, 0, has_up)):
        @pl.when(cond)
        def _():
            for g in range(groups):
                for n, ret in enumerate((k_ret, v_ret)):
                    got(ret.at[slab, :, pl.ds(g * gcols, gcols)], rz_s.at[there, g, n], rz_r.at[there, g, n])
    for out, mid, ret in ((dk_out, k_mid, k_ret), (dv_out, v_mid, v_ret)):
        out[...] = (mid[...] + ret[0].astype(F32) + ret[1].astype(F32)).astype(BF16)

    for step in range(1, nz):
        zf = lax.rem(z + nz - step, nz)
        theirs = t_all.at[c, row_block(zf, share)]
        got(theirs, tg_s.at[step], tg_r.at[step])
        send(None, lambda theirs=theirs, step=step: copy(theirs, theirs, tf_s.at[step], tf_r.at[step], partner))
    for step in range(nz):
        zf = lax.rem(z + nz - step, nz)
        got(t_all.at[1 - c, row_block(zf, share)], tf_s.at[step], tf_r.at[step])
    dtk_out[...] = t_all[0].astype(F32)
    dtv_out[...] = t_all[1].astype(F32)

    for when, make in sent:
        if when is None:
            make().wait_send()
        else:
            pl.when(when)(lambda make=make: make().wait_send())


def per_device(
    mesh_shape, queries, key_rows, value_rows, out_grad, w_out, text_keys, text_values, text_count, window_start
):
    frames, height, width, cols = queries.shape
    rows = frames * height * width
    nz, nx = mesh_shape["seq"], mesh_shape["head"]
    txt = text_keys.shape[0]
    heads = cols // HDIM
    groups = min(4, heads)
    model = w_out.shape[0]
    chunk = model // (2 * nz)
    key = np.arange(6 * rows)
    block, inner = key // rows, key % rows
    half, slab = block // 3, block % 3
    table = np.zeros((8, 6 * rows), np.int32)
    table[0] = (slab - 1) * frames + inner // (height * width)
    table[1] = (half * height + inner // width % height) // TH
    table[2] = inner % width // TW
    own = np.arange(rows)
    tiles_w = width // TW
    tile = (own // (height * width) * (height // TH) + own // width % height // TH) * tiles_w + own % width // TW
    tile = tile.astype(np.int32)[:, None]
    dma = pltpu.SemaphoreType.DMA
    vmem = pltpu.VMEM
    anywhere = pl.BlockSpec(memory_space=pl.ANY)
    in_vmem = pl.BlockSpec(memory_space=pltpu.VMEM)
    in_smem = pl.BlockSpec(memory_space=pltpu.SMEM)
    flat = (rows, cols)
    cfg = (nz, nx, rows, cols, groups, frames, height, width)
    out = pl.pallas_call(
        functools.partial(body, cfg),
        in_specs=[in_smem, in_smem, in_vmem, in_vmem] + [anywhere] * 7,
        out_specs=[in_vmem] * 6,
        out_shape=[
            jax.ShapeDtypeStruct(flat, BF16), jax.ShapeDtypeStruct(flat, BF16), jax.ShapeDtypeStruct(flat, BF16),
            jax.ShapeDtypeStruct((chunk, cols), F32),
            jax.ShapeDtypeStruct((txt, cols), F32), jax.ShapeDtypeStruct((txt, cols), F32),
        ],
        scratch_shapes=[
            vmem(flat, BF16), vmem((txt, cols), BF16), vmem((txt, cols), BF16), vmem((model, cols), BF16),
            vmem(flat, BF16), vmem((rows, 6 * rows + txt), F32),
            vmem((nx, rows, model // nx), BF16), vmem((2 * nz, rows, chunk), BF16), vmem((nz, 2 * rows, chunk), BF16),
            vmem((6 * rows, cols), BF16), vmem((6 * rows, cols), BF16),
            vmem((6 * rows, cols), BF16), vmem((6 * rows, cols), BF16),
            vmem((3 * rows, cols), BF16), vmem((3 * rows, cols), BF16),
            vmem((2, rows, cols), BF16), vmem((2, rows, cols), BF16),
            vmem(flat, F32), vmem(flat, F32),
            vmem((2, rows, cols), BF16), vmem((2, rows, cols), BF16),
            vmem((nz, 2 * rows, cols), BF16),
            vmem((2, txt, cols), BF16), vmem((txt, cols), BF16), vmem((txt, cols), BF16), vmem((txt, cols), BF16),
            vmem((2, txt, cols), BF16),
            dma((7,)), dma((nx,)), dma((nx,)), dma((2, 2)), dma((2, 2)), dma((3, 2)), dma((3, 2)),
            dma((nz, 2)), dma((nz, 2)), dma((groups, 2)), dma((groups, 2)), dma((2, groups, 2)), dma((2, groups, 2)),
            dma((groups, nz)), dma((groups, nz)), dma((groups, nz)), dma((groups, nz)),
            dma, dma, dma((nz,)), dma((nz,)), dma((nz,)), dma((nz,)), dma((nz,)), dma((nz,)),
        ],
        compiler_params=pltpu.CompilerParams(
            collective_id=0, has_side_effects=True, vmem_limit_bytes=62 * 1024 * 1024),
        name="sta_backward",
    )(window_start.reshape(-1), text_count, jnp.asarray(table), jnp.asarray(tile),
      queries.reshape(flat), key_rows.reshape(flat), value_rows.reshape(flat), out_grad.reshape(rows, -1),
      w_out, text_keys, text_values)
    dq, dk, dv, gw, dtk, dtv = out
    return dq.reshape(queries.shape), dk.reshape(queries.shape), dv.reshape(queries.shape), gw, dtk, dtv


def solution(mesh):
    tok = P(("parts", "seq"), "hgt", None, "head")
    return jax.shard_map(
        functools.partial(per_device, dict(mesh.shape)),
        mesh=mesh,
        in_specs=(tok, tok, tok, tok, P(None, "head"), P("parts", "head"), P("parts", "head"),
                  P("parts"), P("parts", None, None, None)),
        out_specs=(tok, tok, tok, P(("parts", "seq", "hgt"), "head"), P("parts", "head"), P("parts", "head")),
        check_vma=False,
    )
```

```python
import functools

import jax
import jax.numpy as jnp
import numpy as np
from jax import lax
from jax.experimental import pallas as pl
from jax.experimental.pallas import tpu as pltpu
from jax.sharding import PartitionSpec as P

HDIM = 128
TH = 2
TW = 8
WIN = 3

F32 = jnp.float32
BF16 = jnp.bfloat16
MESH = pl.DeviceIdType.MESH


def contract(a, b, dims):
    return lax.dot_general(a, b, (dims, ((), ())), preferred_element_type=F32)


def body(cfg, window, count, key_table, tile_table, q_in, k_in, v_in, og_in, w_in, tk_in, tv_in,
         dq_out, dk_out, dv_out, gw_out, dtk_out, dtv_out,
         q, tk, tv, w, do, bias, gfull, stage, a_all, k_ext, v_ext, dk_part, dv_part, k_got, v_got,
         k_sum, v_sum, k_mid, v_mid, k_ret, v_ret, o_all, t_part, t_got, t_sum, t_red, t_all,
         loc, og_s, og_r, kv_s, kv_r, kp_s, kp_r, a_s, a_r, ax_s, ax_r, pr_s, pr_r, rz_s, rz_r,
         o_s, o_r, of_s, of_r, tp_s, tp_r, ts_s, ts_r, tg_s, tg_r, tf_s, tf_r):
    nz, nx, rows, cols, groups, frames, height, width = cfg
    txt = tk_in.shape[0]
    slot = og_in.shape[1]
    chunk = stage.shape[2]
    share = txt // nz
    ext = 6 * rows
    heads = cols // HDIM
    per = heads // groups
    gcols = per * HDIM
    scale = HDIM ** -0.5
    y, z, x, c = (lax.axis_index(n) for n in ("parts", "seq", "head", "hgt"))
    partner = (y, z, x, 1 - c)
    up = (y, lax.rem(z + 1, nz), x, c)
    down = (y, lax.rem(z + nz - 1, nz), x, c)
    split = 2 if nx % 2 == 0 else 1
    piece = rows // split
    x_half = lax.rem(x, split)
    x_partner = (y, z, x + 1 - 2 * x_half, c)
    has_up = z < nz - 1
    has_down = z > 0

    def seq_peer(step):
        zt = lax.rem(z + step, nz)
        return zt, (y, zt, x, c)

    def copy(src, dst, s, r, dev):
        return pltpu.make_async_remote_copy(
            src_ref=src, dst_ref=dst, send_sem=s, recv_sem=r, device_id=dev, device_id_type=MESH)

    def got(dst, s, r):
        copy(dst, dst, s, r, partner).wait_recv()

    def row_block(n, size):
        return pl.ds(pl.multiple_of(n * size, 16), size)

    def key_rows(half, slab):
        return row_block(half * 3 + slab, rows)

    def a_piece(zf, cf, n):
        return a_all.at[zf, pl.ds(pl.multiple_of(cf * rows + n * piece, 16), piece), :]

    sent = []

    def send(when, make):
        if when is None:
            make().start()
        else:
            pl.when(when)(lambda: make().start())
        sent.append((when, make))

    locals_ = [
        pltpu.make_async_copy(w_in, w, loc.at[0]),
        pltpu.make_async_copy(q_in, q, loc.at[1]),
        pltpu.make_async_copy(tk_in, tk, loc.at[2]),
        pltpu.make_async_copy(tv_in, tv, loc.at[3]),
        pltpu.make_async_copy(k_in, k_ext.at[key_rows(c, 1)], loc.at[4]),
        pltpu.make_async_copy(v_in, v_ext.at[key_rows(c, 1)], loc.at[5]),
        pltpu.make_async_copy(og_in, gfull.at[x], loc.at[6]),
    ]
    locals_[6].start()
    for n in range(6):
        locals_[n].start()

    barrier = pltpu.get_barrier_semaphore()
    for step in range(nz):
        zt, dev = seq_peer(step)
        if step:
            pl.semaphore_signal(barrier, inc=1, device_id=dev, device_id_type=MESH)
        pl.semaphore_signal(barrier, inc=1, device_id=(y, zt, x, 1 - c), device_id_type=MESH)
    for step in range(1, nx):
        pl.semaphore_signal(barrier, inc=1, device_id=(y, z, lax.rem(x + step, nx), c), device_id_type=MESH)
    pl.semaphore_wait(barrier, 2 * nz - 1 + nx - 1)

    for step in range(1, nx):
        send(None, lambda step=step: copy(og_in, gfull.at[x], og_s.at[step], og_r.at[step],
                                          (y, z, lax.rem(x + step, nx), c)))
    for n, (src, dst) in enumerate(((k_in, k_ext), (v_in, v_ext))):
        send(has_up, lambda n=n, src=src, dst=dst: copy(
            src, dst.at[key_rows(c, 0)], kv_s.at[0, n], kv_r.at[0, n], up))
        send(has_down, lambda n=n, src=src, dst=dst: copy(
            src, dst.at[key_rows(c, 2)], kv_s.at[1, n], kv_r.at[1, n], down))
    for n, (src, dst) in enumerate(((k_in, k_ext), (v_in, v_ext))):
        send(None, lambda n=n, src=src, dst=dst: copy(
            src, dst.at[key_rows(c, 1)], kp_s.at[1, n], kp_r.at[1, n], partner))

    @pl.when(jnp.logical_not(has_down))
    def _():
        for ref in (k_ext, v_ext):
            for half in range(2):
                ref[pl.ds(half * 3 * rows, rows), :] = jnp.zeros((rows, cols), BF16)
        for ref in (k_ret, v_ret):
            ref[0] = jnp.zeros((rows, cols), BF16)

    @pl.when(jnp.logical_not(has_up))
    def _():
        for ref in (k_ext, v_ext):
            for half in range(2):
                ref[pl.ds((half * 3 + 2) * rows, rows), :] = jnp.zeros((rows, cols), BF16)
        for ref in (k_ret, v_ret):
            ref[1] = jnp.zeros((rows, cols), BF16)

    tile_id = tile_table[...]
    tiles_h, tiles_w = 2 * height // TH, width // TW
    ok = None
    for n in range(3):
        low = jnp.zeros((rows, 1), jnp.int32)
        t = 0
        for f in range(frames):
            for r in range(height // TH):
                for e in range(tiles_w):
                    at = (((z * frames + f) * tiles_h + c * (height // TH) + r) * tiles_w + e) * 3 + n
                    low = jnp.where(tile_id == t, window[at], low)
                    t += 1
        pos = key_table[n:n + 1, :]
        if n == 0:
            pos = pos + z * frames
        term = (pos >= low) & (pos < low + WIN)
        ok = term if ok is None else ok & term
    bias[:, :ext] = jnp.where(ok, F32(0), F32(-jnp.inf))
    place = lax.broadcasted_iota(jnp.int32, (rows, txt), 1)
    bias[:, ext:] = jnp.where(place < count[0], F32(0), F32(-jnp.inf))

    locals_[0].wait()
    locals_[6].wait()

    def term_of(xs):
        return contract(gfull[xs], w[row_block(xs, slot), :], ((1,), (0,)))

    total = term_of(x)
    for step in range(1, nx):
        xs = lax.rem(x + nx - step, nx)
        got(gfull.at[xs], og_s.at[step], og_r.at[step])
    per_slot = slot // chunk
    for j in range(2 * nz):
        stage[j] = gfull[j // per_slot, :, (j % per_slot) * chunk:(j % per_slot + 1) * chunk]
    for step in range(1, nz):
        for ct in range(2):
            zt = lax.rem(z + step, nz)
            send(None, lambda zt=zt, step=step, ct=ct: copy(
                stage.at[zt * 2 + ct, row_block(x_half, piece), :], a_piece(z, c, x_half), a_s.at[step, ct],
                a_r.at[step, c], (y, zt, x, ct)))
    send(None, lambda: copy(stage.at[z * 2 + 1 - c], a_all.at[z, row_block(c, rows), :], a_s.at[0, 0], a_r.at[0, c],
                            partner))
    a_all[z, row_block(c, rows), :] = stage[z * 2 + c]

    for slab, there, cond in ((0, 0, has_down), (2, 1, has_up)):
        @pl.when(cond)
        def _():
            for n, dst in enumerate((k_ext, v_ext)):
                got(dst.at[key_rows(c, slab)], kv_s.at[there, n], kv_r.at[there, n])
        for n, dst in enumerate((k_ext, v_ext)):
            send(cond, lambda n=n, dst=dst, slab=slab: copy(
                dst.at[key_rows(c, slab)], dst.at[key_rows(c, slab)], kp_s.at[slab, n], kp_r.at[slab, n], partner))

    for step in range(1, nx):
        total = total + term_of(lax.rem(x + nx - step, nx))
    do[...] = total.astype(BF16)

    for n in range(1, 6):
        locals_[n].wait()
    for slab, cond in ((0, has_down), (1, None), (2, has_up)):
        def arrive(slab=slab):
            for n, dst in enumerate((k_ext, v_ext)):
                got(dst.at[key_rows(1 - c, slab)], kp_s.at[slab, n], kp_r.at[slab, n])
        if cond is None:
            arrive()
        else:
            pl.when(cond)(arrive)

    def reduce_group(g):
        lanes = pl.ds(g * gcols, gcols)
        for n, (part, have, mid, summed, ret) in enumerate((
                (dk_part, k_got, k_mid, k_sum, k_ret), (dv_part, v_got, v_mid, v_sum, v_ret))):
            got(have.at[:, lanes], pr_s.at[g, n], pr_r.at[g, n])
            for slab in range(3):
                value = (part[key_rows(c, slab), lanes].astype(F32)
                         + have[pl.ds(slab * rows, rows), lanes].astype(F32))
                if slab == 1:
                    mid[:, lanes] = value
                else:
                    summed[slab // 2, :, lanes] = value.astype(BF16)
            send(has_down, lambda n=n, summed=summed, ret=ret: copy(
                summed.at[0, :, lanes], ret.at[1, :, lanes], rz_s.at[0, g, n], rz_r.at[0, g, n], down))
            send(has_up, lambda n=n, summed=summed, ret=ret: copy(
                summed.at[1, :, lanes], ret.at[0, :, lanes], rz_s.at[1, g, n], rz_r.at[1, g, n], up))

    def share_pieces(step):
        zf = lax.rem(z + nz - step, nz)
        for cf in range(2):
            theirs = a_piece(zf, cf, x_half)
            got(theirs, a_s.at[step, cf], a_r.at[step, cf])
            if split > 1:
                send(None, lambda theirs=theirs, cf=cf: copy(
                    theirs, theirs, ax_s.at[step, cf], ax_r.at[step, cf], x_partner))

    for g in range(groups):
        for h in range(g * per, (g + 1) * per):
            at = pl.ds(h * HDIM, HDIM)
            qh, doh, kh, vh, tkh, tvh = q[:, at], do[:, at], k_ext[:, at], v_ext[:, at], tk[:, at], tv[:, at]
            s_w = contract(qh, kh, ((1,), (1,))) * scale + bias[:, :ext]
            s_t = contract(qh, tkh, ((1,), (1,))) * scale + bias[:, ext:]
            top = jnp.maximum(jnp.max(s_w, axis=1, keepdims=True), jnp.max(s_t, axis=1, keepdims=True))
            e_w = jnp.exp(s_w - top)
            e_t = jnp.exp(s_t - top)
            inv = 1.0 / (jnp.sum(e_w, axis=1, keepdims=True) + jnp.sum(e_t, axis=1, keepdims=True))
            p_w = e_w * inv
            p_t = e_t * inv
            pb_w = p_w.astype(BF16)
            pb_t = p_t.astype(BF16)
            oh = (contract(pb_w, vh, ((1,), (0,))) + contract(pb_t, tvh, ((1,), (0,)))).astype(BF16)
            o_all[z, row_block(c, rows), at] = oh
            delta = jnp.sum(doh.astype(F32) * oh.astype(F32), axis=1, keepdims=True)
            ds_w = (p_w * (contract(doh, vh, ((1,), (1,))) - delta)).astype(BF16)
            ds_t = (p_t * (contract(doh, tvh, ((1,), (1,))) - delta)).astype(BF16)
            dq = contract(ds_w, kh, ((1,), (0,))) + contract(ds_t, tkh, ((1,), (0,)))
            dq_out[:, at] = (dq * scale).astype(BF16)
            dk_part[:, at] = (contract(ds_w, qh, ((0,), (0,))) * scale).astype(BF16)
            dv_part[:, at] = contract(pb_w, doh, ((0,), (0,))).astype(BF16)
            t_part[0, :, at] = (contract(ds_t, qh, ((0,), (0,))) * scale).astype(BF16)
            t_part[1, :, at] = contract(pb_t, doh, ((0,), (0,))).astype(BF16)
        lanes = pl.ds(g * gcols, gcols)
        for n, (part, have) in enumerate(((dk_part, k_got), (dv_part, v_got))):
            send(None, lambda n=n, part=part, have=have, g=g, lanes=lanes: copy(
                part.at[row_block(1 - c, 3 * rows), lanes], have.at[:, lanes], pr_s.at[g, n], pr_r.at[g, n], partner))
        for step in range(nz):
            zt, dev = seq_peer(step)
            mine = o_all.at[z, row_block(c, rows), lanes]
            if step:
                send(None, lambda mine=mine, g=g, step=step, dev=dev: copy(
                    mine, mine, o_s.at[g, step], o_r.at[g, step], dev))
            else:
                send(None, lambda mine=mine, g=g: copy(mine, mine, of_s.at[g, 0], of_r.at[g, 0], partner))
        if g:
            reduce_group(g - 1)
        for step in range(1, nz):
            if g == min(step, groups - 1):
                share_pieces(step)

    send(None, lambda: copy(t_part.at[1 - c], t_got, tp_s, tp_r, partner))
    reduce_group(groups - 1)
    got(t_got, tp_s, tp_r)
    t_sum[...] = (t_part[c].astype(F32) + t_got[...].astype(F32)).astype(BF16)
    for step in range(1, nz):
        zt, dev = seq_peer(step)
        send(None, lambda step=step, zt=zt, dev=dev: copy(
            t_sum.at[row_block(zt, share)], t_red.at[row_block(z, share)], ts_s.at[step], ts_r.at[step], dev))

    def share_o(g, step):
        zf = lax.rem(z + nz - step, nz)
        theirs = o_all.at[zf, row_block(c, rows), pl.ds(g * gcols, gcols)]
        got(theirs, o_s.at[g, step], o_r.at[g, step])
        send(None, lambda: copy(theirs, theirs, of_s.at[g, step], of_r.at[g, step], partner))

    def project(step):
        zf = lax.rem(z + nz - step, nz)
        if step == 0:
            got(a_all.at[z, row_block(1 - c, rows), :], a_s.at[0, 0], a_r.at[0, 1 - c])
        elif split > 1:
            for cf in range(2):
                got(a_piece(zf, cf, 1 - x_half), ax_s.at[step, cf], ax_r.at[step, cf])
        for g in range(groups):
            got(o_all.at[zf, row_block(1 - c, rows), pl.ds(g * gcols, gcols)], of_s.at[g, step], of_r.at[g, step])
        part = contract(a_all[zf], o_all[zf], ((0,), (0,)))
        if step == 0:
            gw_out[...] = part
        else:
            gw_out[...] += part

    for g in range(groups - 1):
        for step in range(1, nz):
            share_o(g, step)

    value = t_sum[row_block(z, share), :].astype(F32)
    for step in range(1, nz):
        zf = lax.rem(z + nz - step, nz)
        got(t_red.at[row_block(zf, share)], ts_s.at[step], ts_r.at[step])
        value = value + t_red[row_block(zf, share), :].astype(F32)
    t_all[c, row_block(z, share), :] = value.astype(BF16)
    own_text = t_all.at[c, row_block(z, share)]
    for step in range(nz):
        zt, dev = seq_peer(step)
        if step:
            send(None, lambda step=step, dev=dev: copy(own_text, own_text, tg_s.at[step], tg_r.at[step], dev))
        else:
            send(None, lambda: copy(own_text, own_text, tf_s.at[0], tf_r.at[0], partner))

    project(0)
    for step in range(1, nz):
        share_o(groups - 1, step)
    for step in range(1, nz):
        project(step)

    for slab, there, cond in ((0, 1, has_down), (1, 0, has_up)):
        @pl.when(cond)
        def _():
            for g in range(groups):
                for n, ret in enumerate((k_ret, v_ret)):
                    got(ret.at[slab, :, pl.ds(g * gcols, gcols)], rz_s.at[there, g, n], rz_r.at[there, g, n])
    for out, mid, ret in ((dk_out, k_mid, k_ret), (dv_out, v_mid, v_ret)):
        out[...] = (mid[...] + ret[0].astype(F32) + ret[1].astype(F32)).astype(BF16)

    for step in range(1, nz):
        zf = lax.rem(z + nz - step, nz)
        theirs = t_all.at[c, row_block(zf, share)]
        got(theirs, tg_s.at[step], tg_r.at[step])
        send(None, lambda theirs=theirs, step=step: copy(theirs, theirs, tf_s.at[step], tf_r.at[step], partner))
    for step in range(nz):
        zf = lax.rem(z + nz - step, nz)
        got(t_all.at[1 - c, row_block(zf, share)], tf_s.at[step], tf_r.at[step])
    dtk_out[...] = t_all[0].astype(F32)
    dtv_out[...] = t_all[1].astype(F32)

    for when, make in sent:
        if when is None:
            make().wait_send()
        else:
            pl.when(when)(lambda make=make: make().wait_send())


def deliver_body(*refs):
    sems = refs[-1]
    count = (len(refs) - 1) // 2
    copies = [pltpu.make_async_copy(refs[n], refs[count + n], sems.at[n]) for n in range(count)]
    for one in copies:
        one.start()
    for one in copies:
        one.wait()


def deliver(arrays):
    anywhere = pl.BlockSpec(memory_space=pl.ANY)
    return pl.pallas_call(
        deliver_body,
        in_specs=[anywhere] * len(arrays),
        out_specs=[anywhere] * len(arrays),
        out_shape=[jax.ShapeDtypeStruct(a.shape, a.dtype) for a in arrays],
        scratch_shapes=[pltpu.SemaphoreType.DMA((len(arrays),))],
        name="deliver",
    )(*arrays)


def per_device(
    mesh_shape, queries, key_rows, value_rows, out_grad, w_out, text_keys, text_values, text_count, window_start
):
    frames, height, width, cols = queries.shape
    rows = frames * height * width
    nz, nx = mesh_shape["seq"], mesh_shape["head"]
    txt = text_keys.shape[0]
    heads = cols // HDIM
    groups = min(4, heads)
    model = w_out.shape[0]
    chunk = model // (2 * nz)
    key = np.arange(6 * rows)
    block, inner = key // rows, key % rows
    half, slab = block // 3, block % 3
    table = np.zeros((8, 6 * rows), np.int32)
    table[0] = (slab - 1) * frames + inner // (height * width)
    table[1] = (half * height + inner // width % height) // TH
    table[2] = inner % width // TW
    own = np.arange(rows)
    tiles_w = width // TW
    tile = (own // (height * width) * (height // TH) + own // width % height // TH) * tiles_w + own % width // TW
    tile = tile.astype(np.int32)[:, None]
    dma = pltpu.SemaphoreType.DMA
    vmem = pltpu.VMEM
    anywhere = pl.BlockSpec(memory_space=pl.ANY)
    in_vmem = pl.BlockSpec(memory_space=pltpu.VMEM)
    in_smem = pl.BlockSpec(memory_space=pltpu.SMEM)
    flat = (rows, cols)
    cfg = (nz, nx, rows, cols, groups, frames, height, width)
    out = pl.pallas_call(
        functools.partial(body, cfg),
        in_specs=[in_smem, in_smem, in_vmem, in_vmem] + [anywhere] * 7,
        out_specs=[in_vmem] * 6,
        out_shape=[
            jax.ShapeDtypeStruct(flat, BF16), jax.ShapeDtypeStruct(flat, BF16), jax.ShapeDtypeStruct(flat, BF16),
            jax.ShapeDtypeStruct((chunk, cols), F32),
            jax.ShapeDtypeStruct((txt, cols), F32), jax.ShapeDtypeStruct((txt, cols), F32),
        ],
        scratch_shapes=[
            vmem(flat, BF16), vmem((txt, cols), BF16), vmem((txt, cols), BF16), vmem((model, cols), BF16),
            vmem(flat, BF16), vmem((rows, 6 * rows + txt), F32),
            vmem((nx, rows, model // nx), BF16), vmem((2 * nz, rows, chunk), BF16), vmem((nz, 2 * rows, chunk), BF16),
            vmem((6 * rows, cols), BF16), vmem((6 * rows, cols), BF16),
            vmem((6 * rows, cols), BF16), vmem((6 * rows, cols), BF16),
            vmem((3 * rows, cols), BF16), vmem((3 * rows, cols), BF16),
            vmem((2, rows, cols), BF16), vmem((2, rows, cols), BF16),
            vmem(flat, F32), vmem(flat, F32),
            vmem((2, rows, cols), BF16), vmem((2, rows, cols), BF16),
            vmem((nz, 2 * rows, cols), BF16),
            vmem((2, txt, cols), BF16), vmem((txt, cols), BF16), vmem((txt, cols), BF16), vmem((txt, cols), BF16),
            vmem((2, txt, cols), BF16),
            dma((7,)), dma((nx,)), dma((nx,)), dma((2, 2)), dma((2, 2)), dma((3, 2)), dma((3, 2)),
            dma((nz, 2)), dma((nz, 2)), dma((nz, 2)), dma((nz, 2)), dma((groups, 2)), dma((groups, 2)), dma((2, groups, 2)), dma((2, groups, 2)),
            dma((groups, nz)), dma((groups, nz)), dma((groups, nz)), dma((groups, nz)),
            dma, dma, dma((nz,)), dma((nz,)), dma((nz,)), dma((nz,)), dma((nz,)), dma((nz,)),
        ],
        compiler_params=pltpu.CompilerParams(
            collective_id=0, has_side_effects=True, vmem_limit_bytes=62 * 1024 * 1024),
        name="sta_backward",
    )(window_start.reshape(-1), text_count, jnp.asarray(table), jnp.asarray(tile),
      queries.reshape(flat), key_rows.reshape(flat), value_rows.reshape(flat), out_grad.reshape(rows, -1),
      w_out, text_keys, text_values)
    dq, dk, dv, gw, dtk, dtv = deliver(out)
    return dq.reshape(queries.shape), dk.reshape(queries.shape), dv.reshape(queries.shape), gw, dtk, dtv


def solution(mesh):
    tok = P(("parts", "seq"), "hgt", None, "head")
    return jax.shard_map(
        functools.partial(per_device, dict(mesh.shape)),
        mesh=mesh,
        in_specs=(tok, tok, tok, tok, P(None, "head"), P("parts", "head"), P("parts", "head"),
                  P("parts"), P("parts", None, None, None)),
        out_specs=(tok, tok, tok, P(("parts", "seq", "hgt"), "head"), P("parts", "head"), P("parts", "head")),
        check_vma=False,
    )
```

```python
import functools

import jax
import jax.numpy as jnp
import numpy as np
from jax import lax
from jax.experimental import pallas as pl
from jax.experimental.pallas import tpu as pltpu
from jax.sharding import PartitionSpec as P

HDIM = 128
TH = 2
TW = 8
WIN = 3

F32 = jnp.float32
BF16 = jnp.bfloat16
MESH = pl.DeviceIdType.MESH


def contract(a, b, dims):
    return lax.dot_general(a, b, (dims, ((), ())), preferred_element_type=F32)


def body(cfg, window, count, key_table, tile_table, q_in, k_in, v_in, og_in, w_in, tk_in, tv_in,
         dq_out, dk_out, dv_out, gw_out, dtk_out, dtv_out,
         q, tk, tv, w, do, bias, gfull, stage, a_all, k_ext, v_ext, dk_part, dv_part, k_got, v_got,
         k_sum, v_sum, k_mid, v_mid, k_ret, v_ret, o_all, t_part, t_got, t_sum, t_red, t_all,
         loc, og_s, og_r, kv_s, kv_r, kp_s, kp_r, a_s, a_r, ax_s, ax_r, pr_s, pr_r, rz_s, rz_r,
         o_s, o_r, of_s, of_r, tp_s, tp_r, ts_s, ts_r, tg_s, tg_r, tf_s, tf_r):
    nz, nx, rows, cols, groups, frames, height, width = cfg
    txt = tk_in.shape[0]
    slot = og_in.shape[1]
    chunk = stage.shape[2]
    share = txt // nz
    ext = 6 * rows
    heads = cols // HDIM
    per = heads // groups
    gcols = per * HDIM
    scale = HDIM ** -0.5
    y, z, x, c = (lax.axis_index(n) for n in ("parts", "seq", "head", "hgt"))
    partner = (y, z, x, 1 - c)
    up = (y, lax.rem(z + 1, nz), x, c)
    down = (y, lax.rem(z + nz - 1, nz), x, c)
    split = 2 if nx % 2 == 0 else 1
    piece = rows // split
    x_half = lax.rem(x, split)
    x_partner = (y, z, x + 1 - 2 * x_half, c)
    has_up = z < nz - 1
    has_down = z > 0

    def seq_peer(step):
        zt = lax.rem(z + step, nz)
        return zt, (y, zt, x, c)

    def copy(src, dst, s, r, dev):
        return pltpu.make_async_remote_copy(
            src_ref=src, dst_ref=dst, send_sem=s, recv_sem=r, device_id=dev, device_id_type=MESH)

    def got(dst, s, r):
        copy(dst, dst, s, r, partner).wait_recv()

    def row_block(n, size):
        return pl.ds(pl.multiple_of(n * size, 16), size)

    def key_rows(half, slab):
        return row_block(half * 3 + slab, rows)

    def a_piece(zf, cf, n):
        return a_all.at[zf, pl.ds(pl.multiple_of(cf * rows + n * piece, 16), piece), :]

    sent = []

    def send(when, make):
        if when is None:
            make().start()
        else:
            pl.when(when)(lambda: make().start())
        sent.append((when, make))

    locals_ = [
        pltpu.make_async_copy(w_in, w, loc.at[0]),
        pltpu.make_async_copy(q_in, q, loc.at[1]),
        pltpu.make_async_copy(tk_in, tk, loc.at[2]),
        pltpu.make_async_copy(tv_in, tv, loc.at[3]),
        pltpu.make_async_copy(k_in, k_ext.at[key_rows(c, 1)], loc.at[4]),
        pltpu.make_async_copy(v_in, v_ext.at[key_rows(c, 1)], loc.at[5]),
        pltpu.make_async_copy(og_in, gfull.at[x], loc.at[6]),
    ]
    locals_[6].start()
    for n in range(6):
        locals_[n].start()

    barrier = pltpu.get_barrier_semaphore()
    for step in range(nz):
        zt, dev = seq_peer(step)
        if step:
            pl.semaphore_signal(barrier, inc=1, device_id=dev, device_id_type=MESH)
        pl.semaphore_signal(barrier, inc=1, device_id=(y, zt, x, 1 - c), device_id_type=MESH)
    for step in range(1, nx):
        pl.semaphore_signal(barrier, inc=1, device_id=(y, z, lax.rem(x + step, nx), c), device_id_type=MESH)
    pl.semaphore_wait(barrier, 2 * nz - 1 + nx - 1)

    for step in range(1, nx):
        send(None, lambda step=step: copy(og_in, gfull.at[x], og_s.at[step], og_r.at[step],
                                          (y, z, lax.rem(x + step, nx), c)))
    for n, (src, dst) in enumerate(((k_in, k_ext), (v_in, v_ext))):
        send(has_up, lambda n=n, src=src, dst=dst: copy(
            src, dst.at[key_rows(c, 0)], kv_s.at[0, n], kv_r.at[0, n], up))
        send(has_down, lambda n=n, src=src, dst=dst: copy(
            src, dst.at[key_rows(c, 2)], kv_s.at[1, n], kv_r.at[1, n], down))
    for n, (src, dst) in enumerate(((k_in, k_ext), (v_in, v_ext))):
        send(None, lambda n=n, src=src, dst=dst: copy(
            src, dst.at[key_rows(c, 1)], kp_s.at[1, n], kp_r.at[1, n], partner))

    @pl.when(jnp.logical_not(has_down))
    def _():
        for ref in (k_ext, v_ext):
            for half in range(2):
                ref[pl.ds(half * 3 * rows, rows), :] = jnp.zeros((rows, cols), BF16)
        for ref in (k_ret, v_ret):
            ref[0] = jnp.zeros((rows, cols), BF16)

    @pl.when(jnp.logical_not(has_up))
    def _():
        for ref in (k_ext, v_ext):
            for half in range(2):
                ref[pl.ds((half * 3 + 2) * rows, rows), :] = jnp.zeros((rows, cols), BF16)
        for ref in (k_ret, v_ret):
            ref[1] = jnp.zeros((rows, cols), BF16)

    tile_id = tile_table[...]
    tiles_h, tiles_w = 2 * height // TH, width // TW
    ok = None
    for n in range(3):
        low = jnp.zeros((rows, 1), jnp.int32)
        t = 0
        for f in range(frames):
            for r in range(height // TH):
                for e in range(tiles_w):
                    at = (((z * frames + f) * tiles_h + c * (height // TH) + r) * tiles_w + e) * 3 + n
                    low = jnp.where(tile_id == t, window[at], low)
                    t += 1
        pos = key_table[n:n + 1, :]
        if n == 0:
            pos = pos + z * frames
        term = (pos >= low) & (pos < low + WIN)
        ok = term if ok is None else ok & term
    bias[:, :ext] = jnp.where(ok, F32(0), F32(-jnp.inf))
    place = lax.broadcasted_iota(jnp.int32, (rows, txt), 1)
    bias[:, ext:] = jnp.where(place < count[0], F32(0), F32(-jnp.inf))

    locals_[0].wait()
    locals_[6].wait()

    def term_of(xs):
        return contract(gfull[xs], w[row_block(xs, slot), :], ((1,), (0,)))

    total = term_of(x)
    for step in range(1, nx):
        xs = lax.rem(x + nx - step, nx)
        got(gfull.at[xs], og_s.at[step], og_r.at[step])
    per_slot = slot // chunk
    for j in range(2 * nz):
        stage[j] = gfull[j // per_slot, :, (j % per_slot) * chunk:(j % per_slot + 1) * chunk]
    for step in range(1, nz):
        for ct in range(2):
            zt = lax.rem(z + step, nz)
            send(None, lambda zt=zt, step=step, ct=ct: copy(
                stage.at[zt * 2 + ct, row_block(x_half, piece), :], a_piece(z, c, x_half), a_s.at[step, ct],
                a_r.at[step, c], (y, zt, x, ct)))
    send(None, lambda: copy(stage.at[z * 2 + 1 - c], a_all.at[z, row_block(c, rows), :], a_s.at[0, 0], a_r.at[0, c],
                            partner))
    a_all[z, row_block(c, rows), :] = stage[z * 2 + c]

    for slab, there, cond in ((0, 0, has_down), (2, 1, has_up)):
        @pl.when(cond)
        def _():
            for n, dst in enumerate((k_ext, v_ext)):
                got(dst.at[key_rows(c, slab)], kv_s.at[there, n], kv_r.at[there, n])
        for n, dst in enumerate((k_ext, v_ext)):
            send(cond, lambda n=n, dst=dst, slab=slab: copy(
                dst.at[key_rows(c, slab)], dst.at[key_rows(c, slab)], kp_s.at[slab, n], kp_r.at[slab, n], partner))

    for step in range(1, nx):
        total = total + term_of(lax.rem(x + nx - step, nx))
    do[...] = total.astype(BF16)

    for n in range(1, 6):
        locals_[n].wait()
    for slab, cond in ((0, has_down), (1, None), (2, has_up)):
        def arrive(slab=slab):
            for n, dst in enumerate((k_ext, v_ext)):
                got(dst.at[key_rows(1 - c, slab)], kp_s.at[slab, n], kp_r.at[slab, n])
        if cond is None:
            arrive()
        else:
            pl.when(cond)(arrive)

    def reduce_group(g):
        lanes = pl.ds(g * gcols, gcols)
        for n, (part, have, mid, summed, ret) in enumerate((
                (dk_part, k_got, k_mid, k_sum, k_ret), (dv_part, v_got, v_mid, v_sum, v_ret))):
            got(have.at[:, lanes], pr_s.at[g, n], pr_r.at[g, n])
            for slab in range(3):
                value = (part[key_rows(c, slab), lanes].astype(F32)
                         + have[pl.ds(slab * rows, rows), lanes].astype(F32))
                if slab == 1:
                    mid[:, lanes] = value
                else:
                    summed[slab // 2, :, lanes] = value.astype(BF16)
            send(has_down, lambda n=n, summed=summed, ret=ret: copy(
                summed.at[0, :, lanes], ret.at[1, :, lanes], rz_s.at[0, g, n], rz_r.at[0, g, n], down))
            send(has_up, lambda n=n, summed=summed, ret=ret: copy(
                summed.at[1, :, lanes], ret.at[0, :, lanes], rz_s.at[1, g, n], rz_r.at[1, g, n], up))

    def share_pieces(step):
        zf = lax.rem(z + nz - step, nz)
        for cf in range(2):
            theirs = a_piece(zf, cf, x_half)
            got(theirs, a_s.at[step, cf], a_r.at[step, cf])
            if split > 1:
                send(None, lambda theirs=theirs, cf=cf: copy(
                    theirs, theirs, ax_s.at[step, cf], ax_r.at[step, cf], x_partner))

    for g in range(groups):
        for h in range(g * per, (g + 1) * per):
            at = pl.ds(h * HDIM, HDIM)
            qh, doh, kh, vh, tkh, tvh = q[:, at], do[:, at], k_ext[:, at], v_ext[:, at], tk[:, at], tv[:, at]
            s_w = contract(qh, kh, ((1,), (1,))) * scale + bias[:, :ext]
            s_t = contract(qh, tkh, ((1,), (1,))) * scale + bias[:, ext:]
            top = jnp.maximum(jnp.max(s_w, axis=1, keepdims=True), jnp.max(s_t, axis=1, keepdims=True))
            e_w = jnp.exp(s_w - top)
            e_t = jnp.exp(s_t - top)
            inv = 1.0 / (jnp.sum(e_w, axis=1, keepdims=True) + jnp.sum(e_t, axis=1, keepdims=True))
            p_w = e_w * inv
            p_t = e_t * inv
            pb_w = p_w.astype(BF16)
            pb_t = p_t.astype(BF16)
            oh = (contract(pb_w, vh, ((1,), (0,))) + contract(pb_t, tvh, ((1,), (0,)))).astype(BF16)
            o_all[z, row_block(c, rows), at] = oh
            delta = jnp.sum(doh.astype(F32) * oh.astype(F32), axis=1, keepdims=True)
            ds_w = (p_w * (contract(doh, vh, ((1,), (1,))) - delta)).astype(BF16)
            ds_t = (p_t * (contract(doh, tvh, ((1,), (1,))) - delta)).astype(BF16)
            dq = contract(ds_w, kh, ((1,), (0,))) + contract(ds_t, tkh, ((1,), (0,)))
            dq_out[:, at] = (dq * scale).astype(BF16)
            dk_part[:, at] = (contract(ds_w, qh, ((0,), (0,))) * scale).astype(BF16)
            dv_part[:, at] = contract(pb_w, doh, ((0,), (0,))).astype(BF16)
            t_part[0, :, at] = (contract(ds_t, qh, ((0,), (0,))) * scale).astype(BF16)
            t_part[1, :, at] = contract(pb_t, doh, ((0,), (0,))).astype(BF16)
        lanes = pl.ds(g * gcols, gcols)
        for n, (part, have) in enumerate(((dk_part, k_got), (dv_part, v_got))):
            send(None, lambda n=n, part=part, have=have, g=g, lanes=lanes: copy(
                part.at[row_block(1 - c, 3 * rows), lanes], have.at[:, lanes], pr_s.at[g, n], pr_r.at[g, n], partner))
        for step in range(nz):
            zt, dev = seq_peer(step)
            mine = o_all.at[z, row_block(c, rows), lanes]
            if step:
                send(None, lambda mine=mine, g=g, step=step, dev=dev: copy(
                    mine, mine, o_s.at[g, step], o_r.at[g, step], dev))
            else:
                send(None, lambda mine=mine, g=g: copy(mine, mine, of_s.at[g, 0], of_r.at[g, 0], partner))
        if g:
            reduce_group(g - 1)
        for step in range(1, nz):
            if g == min(step, groups - 1):
                share_pieces(step)

    send(None, lambda: copy(t_part.at[1 - c], t_got, tp_s, tp_r, partner))
    reduce_group(groups - 1)
    got(t_got, tp_s, tp_r)
    t_sum[...] = (t_part[c].astype(F32) + t_got[...].astype(F32)).astype(BF16)
    for step in range(1, nz):
        zt, dev = seq_peer(step)
        send(None, lambda step=step, zt=zt, dev=dev: copy(
            t_sum.at[row_block(zt, share)], t_red.at[row_block(z, share)], ts_s.at[step], ts_r.at[step], dev))

    def share_o(g, step):
        zf = lax.rem(z + nz - step, nz)
        theirs = o_all.at[zf, row_block(c, rows), pl.ds(g * gcols, gcols)]
        got(theirs, o_s.at[g, step], o_r.at[g, step])
        send(None, lambda: copy(theirs, theirs, of_s.at[g, step], of_r.at[g, step], partner))

    def project(step):
        zf = lax.rem(z + nz - step, nz)
        if step == 0:
            got(a_all.at[z, row_block(1 - c, rows), :], a_s.at[0, 0], a_r.at[0, 1 - c])
        elif split > 1:
            for cf in range(2):
                got(a_piece(zf, cf, 1 - x_half), ax_s.at[step, cf], ax_r.at[step, cf])
        for g in range(groups):
            got(o_all.at[zf, row_block(1 - c, rows), pl.ds(g * gcols, gcols)], of_s.at[g, step], of_r.at[g, step])
        part = contract(a_all[zf], o_all[zf], ((0,), (0,)))
        if step == 0:
            gw_out[...] = part
        else:
            gw_out[...] += part

    for g in range(groups - 1):
        for step in range(1, nz):
            share_o(g, step)

    value = t_sum[row_block(z, share), :].astype(F32)
    for step in range(1, nz):
        zf = lax.rem(z + nz - step, nz)
        got(t_red.at[row_block(zf, share)], ts_s.at[step], ts_r.at[step])
        value = value + t_red[row_block(zf, share), :].astype(F32)
    t_all[c, row_block(z, share), :] = value.astype(BF16)
    own_text = t_all.at[c, row_block(z, share)]
    for step in range(nz):
        zt, dev = seq_peer(step)
        if step:
            send(None, lambda step=step, dev=dev: copy(own_text, own_text, tg_s.at[step], tg_r.at[step], dev))
        else:
            send(None, lambda: copy(own_text, own_text, tf_s.at[0], tf_r.at[0], partner))

    project(0)
    for step in range(1, nz):
        share_o(groups - 1, step)
    for step in range(1, nz):
        project(step)

    for slab, there, cond in ((0, 1, has_down), (1, 0, has_up)):
        @pl.when(cond)
        def _():
            for g in range(groups):
                for n, ret in enumerate((k_ret, v_ret)):
                    got(ret.at[slab, :, pl.ds(g * gcols, gcols)], rz_s.at[there, g, n], rz_r.at[there, g, n])
    for out, mid, ret in ((dk_out, k_mid, k_ret), (dv_out, v_mid, v_ret)):
        out[...] = (mid[...] + ret[0].astype(F32) + ret[1].astype(F32)).astype(BF16)

    for step in range(1, nz):
        zf = lax.rem(z + nz - step, nz)
        theirs = t_all.at[c, row_block(zf, share)]
        got(theirs, tg_s.at[step], tg_r.at[step])
        send(None, lambda theirs=theirs, step=step: copy(theirs, theirs, tf_s.at[step], tf_r.at[step], partner))
    for step in range(nz):
        zf = lax.rem(z + nz - step, nz)
        got(t_all.at[1 - c, row_block(zf, share)], tf_s.at[step], tf_r.at[step])
    dtk_out[...] = t_all[0].astype(F32)
    dtv_out[...] = t_all[1].astype(F32)

    for when, make in sent:
        if when is None:
            make().wait_send()
        else:
            pl.when(when)(lambda make=make: make().wait_send())


def deliver_body(*refs):
    count = (len(refs) - 2) // 3
    source, target, held = refs[:count], refs[count:2 * count], refs[2 * count:3 * count]
    in_sem, out_sem = refs[-2:]
    come = [pltpu.make_async_copy(source[n], held[n], in_sem.at[n]) for n in range(count)]
    go = [pltpu.make_async_copy(held[n], target[n], out_sem.at[n]) for n in range(count)]
    for one in come:
        one.start()
    for n in range(count):
        come[n].wait()
        go[n].start()
    for one in go:
        one.wait()


def deliver(arrays):
    anywhere = pl.BlockSpec(memory_space=pl.ANY)
    sems = pltpu.SemaphoreType.DMA((len(arrays),))
    return pl.pallas_call(
        deliver_body,
        in_specs=[anywhere] * len(arrays),
        out_specs=[anywhere] * len(arrays),
        out_shape=[jax.ShapeDtypeStruct(a.shape, a.dtype) for a in arrays],
        scratch_shapes=[pltpu.VMEM(a.shape, a.dtype) for a in arrays] + [sems, sems],
        compiler_params=pltpu.CompilerParams(vmem_limit_bytes=62 * 1024 * 1024),
        name="deliver",
    )(*arrays)


def per_device(
    mesh_shape, queries, key_rows, value_rows, out_grad, w_out, text_keys, text_values, text_count, window_start
):
    frames, height, width, cols = queries.shape
    rows = frames * height * width
    nz, nx = mesh_shape["seq"], mesh_shape["head"]
    txt = text_keys.shape[0]
    heads = cols // HDIM
    groups = min(4, heads)
    model = w_out.shape[0]
    chunk = model // (2 * nz)
    key = np.arange(6 * rows)
    block, inner = key // rows, key % rows
    half, slab = block // 3, block % 3
    table = np.zeros((8, 6 * rows), np.int32)
    table[0] = (slab - 1) * frames + inner // (height * width)
    table[1] = (half * height + inner // width % height) // TH
    table[2] = inner % width // TW
    own = np.arange(rows)
    tiles_w = width // TW
    tile = (own // (height * width) * (height // TH) + own // width % height // TH) * tiles_w + own % width // TW
    tile = tile.astype(np.int32)[:, None]
    dma = pltpu.SemaphoreType.DMA
    vmem = pltpu.VMEM
    anywhere = pl.BlockSpec(memory_space=pl.ANY)
    in_vmem = pl.BlockSpec(memory_space=pltpu.VMEM)
    in_smem = pl.BlockSpec(memory_space=pltpu.SMEM)
    flat = (rows, cols)
    cfg = (nz, nx, rows, cols, groups, frames, height, width)
    out = pl.pallas_call(
        functools.partial(body, cfg),
        in_specs=[in_smem, in_smem, in_vmem, in_vmem] + [anywhere] * 7,
        out_specs=[in_vmem] * 6,
        out_shape=[
            jax.ShapeDtypeStruct(flat, BF16), jax.ShapeDtypeStruct(flat, BF16), jax.ShapeDtypeStruct(flat, BF16),
            jax.ShapeDtypeStruct((chunk, cols), F32),
            jax.ShapeDtypeStruct((txt, cols), F32), jax.ShapeDtypeStruct((txt, cols), F32),
        ],
        scratch_shapes=[
            vmem(flat, BF16), vmem((txt, cols), BF16), vmem((txt, cols), BF16), vmem((model, cols), BF16),
            vmem(flat, BF16), vmem((rows, 6 * rows + txt), F32),
            vmem((nx, rows, model // nx), BF16), vmem((2 * nz, rows, chunk), BF16), vmem((nz, 2 * rows, chunk), BF16),
            vmem((6 * rows, cols), BF16), vmem((6 * rows, cols), BF16),
            vmem((6 * rows, cols), BF16), vmem((6 * rows, cols), BF16),
            vmem((3 * rows, cols), BF16), vmem((3 * rows, cols), BF16),
            vmem((2, rows, cols), BF16), vmem((2, rows, cols), BF16),
            vmem(flat, F32), vmem(flat, F32),
            vmem((2, rows, cols), BF16), vmem((2, rows, cols), BF16),
            vmem((nz, 2 * rows, cols), BF16),
            vmem((2, txt, cols), BF16), vmem((txt, cols), BF16), vmem((txt, cols), BF16), vmem((txt, cols), BF16),
            vmem((2, txt, cols), BF16),
            dma((7,)), dma((nx,)), dma((nx,)), dma((2, 2)), dma((2, 2)), dma((3, 2)), dma((3, 2)),
            dma((nz, 2)), dma((nz, 2)), dma((nz, 2)), dma((nz, 2)), dma((groups, 2)), dma((groups, 2)), dma((2, groups, 2)), dma((2, groups, 2)),
            dma((groups, nz)), dma((groups, nz)), dma((groups, nz)), dma((groups, nz)),
            dma, dma, dma((nz,)), dma((nz,)), dma((nz,)), dma((nz,)), dma((nz,)), dma((nz,)),
        ],
        compiler_params=pltpu.CompilerParams(
            collective_id=0, has_side_effects=True, vmem_limit_bytes=62 * 1024 * 1024),
        name="sta_backward",
    )(window_start.reshape(-1), text_count, jnp.asarray(table), jnp.asarray(tile),
      queries.reshape(flat), key_rows.reshape(flat), value_rows.reshape(flat), out_grad.reshape(rows, -1),
      w_out, text_keys, text_values)
    dq, dk, dv, gw, dtk, dtv = deliver(out)
    return dq.reshape(queries.shape), dk.reshape(queries.shape), dv.reshape(queries.shape), gw, dtk, dtv


def solution(mesh):
    tok = P(("parts", "seq"), "hgt", None, "head")
    return jax.shard_map(
        functools.partial(per_device, dict(mesh.shape)),
        mesh=mesh,
        in_specs=(tok, tok, tok, tok, P(None, "head"), P("parts", "head"), P("parts", "head"),
                  P("parts"), P("parts", None, None, None)),
        out_specs=(tok, tok, tok, P(("parts", "seq", "hgt"), "head"), P("parts", "head"), P("parts", "head")),
        check_vma=False,
    )
```

```python
import functools

import jax
import jax.numpy as jnp
import numpy as np
from jax import lax
from jax.experimental import pallas as pl
from jax.experimental.pallas import tpu as pltpu
from jax.sharding import PartitionSpec as P

HDIM = 128
TH = 2
TW = 8
WIN = 3

F32 = jnp.float32
BF16 = jnp.bfloat16
MESH = pl.DeviceIdType.MESH


def contract(a, b, dims):
    return lax.dot_general(a, b, (dims, ((), ())), preferred_element_type=F32)


def body(cfg, window, count, key_table, tile_table, q_in, k_in, v_in, og_in, w_in, tk_in, tv_in,
         dq_out, dk_out, dv_out, gw_out, dtk_out, dtv_out,
         q, tk, tv, w, do, bias, gfull, stage, a_all, k_ext, v_ext, dk_part, dv_part, k_got, v_got,
         k_sum, v_sum, k_mid, v_mid, k_ret, v_ret, o_all, t_part, t_got, t_sum, t_red, t_run, t_all,
         loc, og_s, og_r, kv_s, kv_r, kp_s, kp_r, a_s, a_r, ax_s, ax_r, pr_s, pr_r, rz_s, rz_r,
         o_s, o_r, of_s, of_r, tp_s, tp_r, ts_s, ts_r, tg_s, tg_r, tf_s, tf_r):
    nz, nx, rows, cols, groups, frames, height, width = cfg
    txt = tk_in.shape[0]
    slot = og_in.shape[1]
    chunk = stage.shape[2]
    share = txt // nz
    ext = 6 * rows
    heads = cols // HDIM
    per = heads // groups
    gcols = per * HDIM
    scale = HDIM ** -0.5
    y, z, x, c = (lax.axis_index(n) for n in ("parts", "seq", "head", "hgt"))
    partner = (y, z, x, 1 - c)
    up = (y, lax.rem(z + 1, nz), x, c)
    down = (y, lax.rem(z + nz - 1, nz), x, c)
    split = 2 if nx % 2 == 0 else 1
    piece = rows // split
    x_half = lax.rem(x, split)
    x_partner = (y, z, x + 1 - 2 * x_half, c)
    has_up = z < nz - 1
    has_down = z > 0

    def seq_peer(step):
        zt = lax.rem(z + step, nz)
        return zt, (y, zt, x, c)

    def copy(src, dst, s, r, dev):
        return pltpu.make_async_remote_copy(
            src_ref=src, dst_ref=dst, send_sem=s, recv_sem=r, device_id=dev, device_id_type=MESH)

    def got(dst, s, r):
        copy(dst, dst, s, r, partner).wait_recv()

    def row_block(n, size):
        return pl.ds(pl.multiple_of(n * size, 16), size)

    def key_rows(half, slab):
        return row_block(half * 3 + slab, rows)

    def a_piece(zf, cf, n):
        return a_all.at[zf, pl.ds(pl.multiple_of(cf * rows + n * piece, 16), piece), :]

    sent = []

    def send(when, make):
        if when is None:
            make().start()
        else:
            pl.when(when)(lambda: make().start())
        sent.append((when, make))

    locals_ = [
        pltpu.make_async_copy(w_in, w, loc.at[0]),
        pltpu.make_async_copy(q_in, q, loc.at[1]),
        pltpu.make_async_copy(tk_in, tk, loc.at[2]),
        pltpu.make_async_copy(tv_in, tv, loc.at[3]),
        pltpu.make_async_copy(k_in, k_ext.at[key_rows(c, 1)], loc.at[4]),
        pltpu.make_async_copy(v_in, v_ext.at[key_rows(c, 1)], loc.at[5]),
        pltpu.make_async_copy(og_in, gfull.at[x], loc.at[6]),
    ]
    locals_[6].start()
    for n in range(6):
        locals_[n].start()

    barrier = pltpu.get_barrier_semaphore()
    for step in range(nz):
        zt, dev = seq_peer(step)
        if step:
            pl.semaphore_signal(barrier, inc=1, device_id=dev, device_id_type=MESH)
        pl.semaphore_signal(barrier, inc=1, device_id=(y, zt, x, 1 - c), device_id_type=MESH)
    for step in range(1, nx):
        pl.semaphore_signal(barrier, inc=1, device_id=(y, z, lax.rem(x + step, nx), c), device_id_type=MESH)
    pl.semaphore_wait(barrier, 2 * nz - 1 + nx - 1)

    for step in range(1, nx):
        send(None, lambda step=step: copy(og_in, gfull.at[x], og_s.at[step], og_r.at[step],
                                          (y, z, lax.rem(x + step, nx), c)))
    for n, (src, dst) in enumerate(((k_in, k_ext), (v_in, v_ext))):
        send(has_up, lambda n=n, src=src, dst=dst: copy(
            src, dst.at[key_rows(c, 0)], kv_s.at[0, n], kv_r.at[0, n], up))
        send(has_down, lambda n=n, src=src, dst=dst: copy(
            src, dst.at[key_rows(c, 2)], kv_s.at[1, n], kv_r.at[1, n], down))
    for n, (src, dst) in enumerate(((k_in, k_ext), (v_in, v_ext))):
        send(None, lambda n=n, src=src, dst=dst: copy(
            src, dst.at[key_rows(c, 1)], kp_s.at[1, n], kp_r.at[1, n], partner))

    @pl.when(jnp.logical_not(has_down))
    def _():
        for ref in (k_ext, v_ext):
            for half in range(2):
                ref[pl.ds(half * 3 * rows, rows), :] = jnp.zeros((rows, cols), BF16)
        for ref in (k_ret, v_ret):
            ref[0] = jnp.zeros((rows, cols), BF16)

    @pl.when(jnp.logical_not(has_up))
    def _():
        for ref in (k_ext, v_ext):
            for half in range(2):
                ref[pl.ds((half * 3 + 2) * rows, rows), :] = jnp.zeros((rows, cols), BF16)
        for ref in (k_ret, v_ret):
            ref[1] = jnp.zeros((rows, cols), BF16)

    tile_id = tile_table[...]
    tiles_h, tiles_w = 2 * height // TH, width // TW
    ok = None
    for n in range(3):
        low = jnp.zeros((rows, 1), jnp.int32)
        t = 0
        for f in range(frames):
            for r in range(height // TH):
                for e in range(tiles_w):
                    at = (((z * frames + f) * tiles_h + c * (height // TH) + r) * tiles_w + e) * 3 + n
                    low = jnp.where(tile_id == t, window[at], low)
                    t += 1
        pos = key_table[n:n + 1, :]
        if n == 0:
            pos = pos + z * frames
        term = (pos >= low) & (pos < low + WIN)
        ok = term if ok is None else ok & term
    bias[:, :ext] = jnp.where(ok, F32(0), F32(-jnp.inf))
    place = lax.broadcasted_iota(jnp.int32, (rows, txt), 1)
    bias[:, ext:] = jnp.where(place < count[0], F32(0), F32(-jnp.inf))

    locals_[0].wait()
    locals_[6].wait()

    def term_of(xs):
        return contract(gfull[xs], w[row_block(xs, slot), :], ((1,), (0,)))

    total = term_of(x)
    for step in range(1, nx):
        xs = lax.rem(x + nx - step, nx)
        got(gfull.at[xs], og_s.at[step], og_r.at[step])
    per_slot = slot // chunk
    for j in range(2 * nz):
        stage[j] = gfull[j // per_slot, :, (j % per_slot) * chunk:(j % per_slot + 1) * chunk]
    for step in range(1, nz):
        for ct in range(2):
            zt = lax.rem(z + step, nz)
            send(None, lambda zt=zt, step=step, ct=ct: copy(
                stage.at[zt * 2 + ct, row_block(x_half, piece), :], a_piece(z, c, x_half), a_s.at[step, ct],
                a_r.at[step, c], (y, zt, x, ct)))
    send(None, lambda: copy(stage.at[z * 2 + 1 - c], a_all.at[z, row_block(c, rows), :], a_s.at[0, 0], a_r.at[0, c],
                            partner))
    a_all[z, row_block(c, rows), :] = stage[z * 2 + c]

    for slab, there, cond in ((0, 0, has_down), (2, 1, has_up)):
        @pl.when(cond)
        def _():
            for n, dst in enumerate((k_ext, v_ext)):
                got(dst.at[key_rows(c, slab)], kv_s.at[there, n], kv_r.at[there, n])
        for n, dst in enumerate((k_ext, v_ext)):
            send(cond, lambda n=n, dst=dst, slab=slab: copy(
                dst.at[key_rows(c, slab)], dst.at[key_rows(c, slab)], kp_s.at[slab, n], kp_r.at[slab, n], partner))

    for step in range(1, nx):
        total = total + term_of(lax.rem(x + nx - step, nx))
    do[...] = total.astype(BF16)

    for n in range(1, 6):
        locals_[n].wait()
    for slab, cond in ((0, has_down), (1, None), (2, has_up)):
        def arrive(slab=slab):
            for n, dst in enumerate((k_ext, v_ext)):
                got(dst.at[key_rows(1 - c, slab)], kp_s.at[slab, n], kp_r.at[slab, n])
        if cond is None:
            arrive()
        else:
            pl.when(cond)(arrive)

    def reduce_group(g):
        lanes = pl.ds(g * gcols, gcols)
        for n, (part, have, mid, summed, ret) in enumerate((
                (dk_part, k_got, k_mid, k_sum, k_ret), (dv_part, v_got, v_mid, v_sum, v_ret))):
            got(have.at[:, lanes], pr_s.at[g, n], pr_r.at[g, n])
            for slab in range(3):
                value = (part[key_rows(c, slab), lanes].astype(F32)
                         + have[pl.ds(slab * rows, rows), lanes].astype(F32))
                if slab == 1:
                    mid[:, lanes] = value
                else:
                    summed[slab // 2, :, lanes] = value.astype(BF16)
            send(has_down, lambda n=n, summed=summed, ret=ret: copy(
                summed.at[0, :, lanes], ret.at[1, :, lanes], rz_s.at[0, g, n], rz_r.at[0, g, n], down))
            send(has_up, lambda n=n, summed=summed, ret=ret: copy(
                summed.at[1, :, lanes], ret.at[0, :, lanes], rz_s.at[1, g, n], rz_r.at[1, g, n], up))

    def share_pieces(step):
        zf = lax.rem(z + nz - step, nz)
        for cf in range(2):
            theirs = a_piece(zf, cf, x_half)
            got(theirs, a_s.at[step, cf], a_r.at[step, cf])
            if split > 1:
                send(None, lambda theirs=theirs, cf=cf: copy(
                    theirs, theirs, ax_s.at[step, cf], ax_r.at[step, cf], x_partner))

    for g in range(groups):
        for h in range(g * per, (g + 1) * per):
            at = pl.ds(h * HDIM, HDIM)
            qh, doh, kh, vh, tkh, tvh = q[:, at], do[:, at], k_ext[:, at], v_ext[:, at], tk[:, at], tv[:, at]
            s_w = contract(qh, kh, ((1,), (1,))) * scale + bias[:, :ext]
            s_t = contract(qh, tkh, ((1,), (1,))) * scale + bias[:, ext:]
            top = jnp.maximum(jnp.max(s_w, axis=1, keepdims=True), jnp.max(s_t, axis=1, keepdims=True))
            e_w = jnp.exp(s_w - top)
            e_t = jnp.exp(s_t - top)
            inv = 1.0 / (jnp.sum(e_w, axis=1, keepdims=True) + jnp.sum(e_t, axis=1, keepdims=True))
            p_w = e_w * inv
            p_t = e_t * inv
            pb_w = p_w.astype(BF16)
            pb_t = p_t.astype(BF16)
            oh = (contract(pb_w, vh, ((1,), (0,))) + contract(pb_t, tvh, ((1,), (0,)))).astype(BF16)
            o_all[z, row_block(c, rows), at] = oh
            delta = jnp.sum(doh.astype(F32) * oh.astype(F32), axis=1, keepdims=True)
            ds_w = (p_w * (contract(doh, vh, ((1,), (1,))) - delta)).astype(BF16)
            ds_t = (p_t * (contract(doh, tvh, ((1,), (1,))) - delta)).astype(BF16)
            dq = contract(ds_w, kh, ((1,), (0,))) + contract(ds_t, tkh, ((1,), (0,)))
            dq_out[:, at] = (dq * scale).astype(BF16)
            dk_part[:, at] = (contract(ds_w, qh, ((0,), (0,))) * scale).astype(BF16)
            dv_part[:, at] = contract(pb_w, doh, ((0,), (0,))).astype(BF16)
            t_part[0, :, at] = (contract(ds_t, qh, ((0,), (0,))) * scale).astype(BF16)
            t_part[1, :, at] = contract(pb_t, doh, ((0,), (0,))).astype(BF16)
        lanes = pl.ds(g * gcols, gcols)
        for n, (part, have) in enumerate(((dk_part, k_got), (dv_part, v_got))):
            send(None, lambda n=n, part=part, have=have, g=g, lanes=lanes: copy(
                part.at[row_block(1 - c, 3 * rows), lanes], have.at[:, lanes], pr_s.at[g, n], pr_r.at[g, n], partner))
        for step in range(nz):
            zt, dev = seq_peer(step)
            mine = o_all.at[z, row_block(c, rows), lanes]
            if step:
                send(None, lambda mine=mine, g=g, step=step, dev=dev: copy(
                    mine, mine, o_s.at[g, step], o_r.at[g, step], dev))
            else:
                send(None, lambda mine=mine, g=g: copy(mine, mine, of_s.at[g, 0], of_r.at[g, 0], partner))
        if g:
            reduce_group(g - 1)
        for step in range(1, nz):
            if g == min(step, groups - 1):
                share_pieces(step)

    send(None, lambda: copy(t_part.at[1 - c], t_got, tp_s, tp_r, partner))
    reduce_group(groups - 1)
    got(t_got, tp_s, tp_r)
    t_sum[...] = (t_part[c].astype(F32) + t_got[...].astype(F32)).astype(BF16)
    for way, first, beyond, dev in ((0, has_down, lambda j: z < j, up), (1, has_up, lambda j: z > j, down)):
        for j in (range(nz - 1, 0, -1) if way == 0 else range(nz - 1)):
            at = pl.ds(j * share, share)

            @pl.when(beyond(j) & first)
            def _():
                got(t_red.at[way, at], ts_s.at[way, j], ts_r.at[way, j])
                t_run[way, at, :] = (t_sum[at, :].astype(F32) + t_red[way, at, :].astype(F32)).astype(BF16)

            @pl.when(beyond(j) & jnp.logical_not(first))
            def _():
                t_run[way, at, :] = t_sum[at, :]

            send(beyond(j), lambda way=way, j=j, at=at, dev=dev: copy(
                t_run.at[way, at], t_red.at[way, at], ts_s.at[way, j], ts_r.at[way, j], dev))

    def share_o(g, step):
        zf = lax.rem(z + nz - step, nz)
        theirs = o_all.at[zf, row_block(c, rows), pl.ds(g * gcols, gcols)]
        got(theirs, o_s.at[g, step], o_r.at[g, step])
        send(None, lambda: copy(theirs, theirs, of_s.at[g, step], of_r.at[g, step], partner))

    def project(step):
        zf = lax.rem(z + nz - step, nz)
        if step == 0:
            got(a_all.at[z, row_block(1 - c, rows), :], a_s.at[0, 0], a_r.at[0, 1 - c])
        elif split > 1:
            for cf in range(2):
                got(a_piece(zf, cf, 1 - x_half), ax_s.at[step, cf], ax_r.at[step, cf])
        for g in range(groups):
            got(o_all.at[zf, row_block(1 - c, rows), pl.ds(g * gcols, gcols)], of_s.at[g, step], of_r.at[g, step])
        part = contract(a_all[zf], o_all[zf], ((0,), (0,)))
        if step == 0:
            gw_out[...] = part
        else:
            gw_out[...] += part

    for g in range(groups - 1):
        for step in range(1, nz):
            share_o(g, step)

    value = t_sum[row_block(z, share), :].astype(F32)
    mine = row_block(z, share)
    for way, cond in ((0, has_down), (1, has_up)):
        @pl.when(cond)
        def _():
            got(t_red.at[way, mine], ts_s.at[way, z], ts_r.at[way, z])

        @pl.when(jnp.logical_not(cond))
        def _():
            t_red[way, mine, :] = jnp.zeros((share, cols), BF16)

        value = value + t_red[way, mine, :].astype(F32)
    t_all[c, mine, :] = value.astype(BF16)
    own_text = t_all.at[c, row_block(z, share)]
    for step in range(nz):
        zt, dev = seq_peer(step)
        if step:
            send(None, lambda step=step, dev=dev: copy(own_text, own_text, tg_s.at[step], tg_r.at[step], dev))
        else:
            send(None, lambda: copy(own_text, own_text, tf_s.at[0], tf_r.at[0], partner))

    project(0)
    for step in range(1, nz):
        share_o(groups - 1, step)
    for step in range(1, nz):
        project(step)

    for slab, there, cond in ((0, 1, has_down), (1, 0, has_up)):
        @pl.when(cond)
        def _():
            for g in range(groups):
                for n, ret in enumerate((k_ret, v_ret)):
                    got(ret.at[slab, :, pl.ds(g * gcols, gcols)], rz_s.at[there, g, n], rz_r.at[there, g, n])
    for out, mid, ret in ((dk_out, k_mid, k_ret), (dv_out, v_mid, v_ret)):
        out[...] = (mid[...] + ret[0].astype(F32) + ret[1].astype(F32)).astype(BF16)

    for step in range(1, nz):
        zf = lax.rem(z + nz - step, nz)
        theirs = t_all.at[c, row_block(zf, share)]
        got(theirs, tg_s.at[step], tg_r.at[step])
        send(None, lambda theirs=theirs, step=step: copy(theirs, theirs, tf_s.at[step], tf_r.at[step], partner))
    for step in range(nz):
        zf = lax.rem(z + nz - step, nz)
        got(t_all.at[1 - c, row_block(zf, share)], tf_s.at[step], tf_r.at[step])
    dtk_out[...] = t_all[0].astype(F32)
    dtv_out[...] = t_all[1].astype(F32)

    for when, make in sent:
        if when is None:
            make().wait_send()
        else:
            pl.when(when)(lambda make=make: make().wait_send())


def deliver_body(*refs):
    count = (len(refs) - 2) // 3
    source, target, held = refs[:count], refs[count:2 * count], refs[2 * count:3 * count]
    in_sem, out_sem = refs[-2:]
    come = [pltpu.make_async_copy(source[n], held[n], in_sem.at[n]) for n in range(count)]
    go = [pltpu.make_async_copy(held[n], target[n], out_sem.at[n]) for n in range(count)]
    for one in come:
        one.start()
    for n in range(count):
        come[n].wait()
        go[n].start()
    for one in go:
        one.wait()


def deliver(arrays):
    anywhere = pl.BlockSpec(memory_space=pl.ANY)
    sems = pltpu.SemaphoreType.DMA((len(arrays),))
    return pl.pallas_call(
        deliver_body,
        in_specs=[anywhere] * len(arrays),
        out_specs=[anywhere] * len(arrays),
        out_shape=[jax.ShapeDtypeStruct(a.shape, a.dtype) for a in arrays],
        scratch_shapes=[pltpu.VMEM(a.shape, a.dtype) for a in arrays] + [sems, sems],
        compiler_params=pltpu.CompilerParams(vmem_limit_bytes=62 * 1024 * 1024),
        name="deliver",
    )(*arrays)


def per_device(
    mesh_shape, queries, key_rows, value_rows, out_grad, w_out, text_keys, text_values, text_count, window_start
):
    frames, height, width, cols = queries.shape
    rows = frames * height * width
    nz, nx = mesh_shape["seq"], mesh_shape["head"]
    txt = text_keys.shape[0]
    heads = cols // HDIM
    groups = min(4, heads)
    model = w_out.shape[0]
    chunk = model // (2 * nz)
    key = np.arange(6 * rows)
    block, inner = key // rows, key % rows
    half, slab = block // 3, block % 3
    table = np.zeros((8, 6 * rows), np.int32)
    table[0] = (slab - 1) * frames + inner // (height * width)
    table[1] = (half * height + inner // width % height) // TH
    table[2] = inner % width // TW
    own = np.arange(rows)
    tiles_w = width // TW
    tile = (own // (height * width) * (height // TH) + own // width % height // TH) * tiles_w + own % width // TW
    tile = tile.astype(np.int32)[:, None]
    dma = pltpu.SemaphoreType.DMA
    vmem = pltpu.VMEM
    anywhere = pl.BlockSpec(memory_space=pl.ANY)
    in_vmem = pl.BlockSpec(memory_space=pltpu.VMEM)
    in_smem = pl.BlockSpec(memory_space=pltpu.SMEM)
    flat = (rows, cols)
    cfg = (nz, nx, rows, cols, groups, frames, height, width)
    out = pl.pallas_call(
        functools.partial(body, cfg),
        in_specs=[in_smem, in_smem, in_vmem, in_vmem] + [anywhere] * 7,
        out_specs=[in_vmem] * 6,
        out_shape=[
            jax.ShapeDtypeStruct(flat, BF16), jax.ShapeDtypeStruct(flat, BF16), jax.ShapeDtypeStruct(flat, BF16),
            jax.ShapeDtypeStruct((chunk, cols), F32),
            jax.ShapeDtypeStruct((txt, cols), F32), jax.ShapeDtypeStruct((txt, cols), F32),
        ],
        scratch_shapes=[
            vmem(flat, BF16), vmem((txt, cols), BF16), vmem((txt, cols), BF16), vmem((model, cols), BF16),
            vmem(flat, BF16), vmem((rows, 6 * rows + txt), F32),
            vmem((nx, rows, model // nx), BF16), vmem((2 * nz, rows, chunk), BF16), vmem((nz, 2 * rows, chunk), BF16),
            vmem((6 * rows, cols), BF16), vmem((6 * rows, cols), BF16),
            vmem((6 * rows, cols), BF16), vmem((6 * rows, cols), BF16),
            vmem((3 * rows, cols), BF16), vmem((3 * rows, cols), BF16),
            vmem((2, rows, cols), BF16), vmem((2, rows, cols), BF16),
            vmem(flat, F32), vmem(flat, F32),
            vmem((2, rows, cols), BF16), vmem((2, rows, cols), BF16),
            vmem((nz, 2 * rows, cols), BF16),
            vmem((2, txt, cols), BF16), vmem((txt, cols), BF16), vmem((txt, cols), BF16), vmem((2, txt, cols), BF16),
            vmem((2, txt, cols), BF16),
            vmem((2, txt, cols), BF16),
            dma((7,)), dma((nx,)), dma((nx,)), dma((2, 2)), dma((2, 2)), dma((3, 2)), dma((3, 2)),
            dma((nz, 2)), dma((nz, 2)), dma((nz, 2)), dma((nz, 2)), dma((groups, 2)), dma((groups, 2)), dma((2, groups, 2)), dma((2, groups, 2)),
            dma((groups, nz)), dma((groups, nz)), dma((groups, nz)), dma((groups, nz)),
            dma, dma, dma((2, nz)), dma((2, nz)), dma((nz,)), dma((nz,)), dma((nz,)), dma((nz,)),
        ],
        compiler_params=pltpu.CompilerParams(
            collective_id=0, has_side_effects=True, vmem_limit_bytes=62 * 1024 * 1024),
        name="sta_backward",
    )(window_start.reshape(-1), text_count, jnp.asarray(table), jnp.asarray(tile),
      queries.reshape(flat), key_rows.reshape(flat), value_rows.reshape(flat), out_grad.reshape(rows, -1),
      w_out, text_keys, text_values)
    dq, dk, dv, gw, dtk, dtv = deliver(out)
    return dq.reshape(queries.shape), dk.reshape(queries.shape), dv.reshape(queries.shape), gw, dtk, dtv


def solution(mesh):
    tok = P(("parts", "seq"), "hgt", None, "head")
    return jax.shard_map(
        functools.partial(per_device, dict(mesh.shape)),
        mesh=mesh,
        in_specs=(tok, tok, tok, tok, P(None, "head"), P("parts", "head"), P("parts", "head"),
                  P("parts"), P("parts", None, None, None)),
        out_specs=(tok, tok, tok, P(("parts", "seq", "hgt"), "head"), P("parts", "head"), P("parts", "head")),
        check_vma=False,
    )
```
